256 devices in a mesh: ctx: 16 (over y, x_hi, core), tp: 16 (over x_lo, z).
Axes of the slice: x: 4 (x_hi: 2, x_lo: 2; x = x_hi * 2 + x_lo), y: 4, z: 8, core: 2. Of those that a mesh axis runs over, the one named last changes fastest.
Arguments:
- prompt_hidden: bfloat16 [1024, 16384], P('ctx', 'tp'), may hold values from -6 to 6
- kv_weight: bfloat16 [16384, 2048], P('tp'), may hold values from -0.046875 to 0.046875
- cache_k: bfloat16 [16384, 1024], P('ctx'), may hold values from -24 to 24
- cache_v: bfloat16 [16384, 1024], P('ctx'), may hold values from -6 to 6
- prompt_q: bfloat16 [1024, 16384], P('ctx', 'tp'), may hold values from -24 to 24
- dec_q: bfloat16 [128, 16384], P('ctx', 'tp'), may hold values from -24 to 24
- dec_k: bfloat16 [128, 1024], P('ctx'), may hold values from -6 to 6
- dec_v: bfloat16 [128, 1024], P('ctx'), may hold values from -6 to 6
- cache_lengths: int32 [16], P('ctx'), may hold values from 1 to 1024, 8192 in all
- prompt_pos: int32 [1024], P('ctx'), may hold values from 0 to 1023, each once
- dec_owner: int32 [128], P('ctx'), may hold values from 0 to 15
Outputs:
- prompt_out: bfloat16 [1024, 16384], P('ctx', 'tp')
- dec_out: bfloat16 [128, 16384], P('ctx', 'tp')
The draws below stay inside these ranges and needn't reach their ends.
Inputs may be any that keep to these rules, and one draw needn't show every extreme that they name: `prompt_pos`: a permutation of the prompt positions.
All inputs are finite; a program needn't handle non-finite values. No bound on the sum of `cache_lengths` on one device may be relied on, other than what follows from the above.
Results may differ from the reference program's by a relative error of at most 0.022.
Values may be sent and summed in bfloat16 or wider, within the bound.
No kernel may reach another device: no remote copies, remote signals or barrier semaphores. Data moves between devices by JAX's collectives and lax.ppermute only.
A program may use at most 128 MiB of HBM per device.

```python
import math
import jax
import jax.numpy as jnp
import numpy as np
from jax import lax

D = 16384
H = 128
KVH = 8
HD = 128
CACHE_DEV = 1024
PROMPT = 1024
CACHE = 16384
DEC = 128
N_CTX = 16


def draw_cache_k(key, part):
    key = jax.random.fold_in(key, 11)
    base = jnp.clip(jax.random.normal(key, (CACHE, KVH * HD), jnp.float32), -6.0, 6.0)
    return base.astype(jnp.bfloat16)


def draw_prompt_q(key, part):
    key = jax.random.fold_in(key, 23)
    base = jnp.clip(jax.random.normal(key, (PROMPT, H * HD), jnp.float32), -6.0, 6.0)
    return base.astype(jnp.bfloat16)


def draw_dec_q(key, part):
    key = jax.random.fold_in(key, 37)
    base = jnp.clip(jax.random.normal(key, (DEC, H * HD), jnp.float32), -6.0, 6.0)
    return base.astype(jnp.bfloat16)


def plant(values, key, least, high):
    longest = values.shape.index(max(values.shape))
    spots = []
    for shift in (0, 1):
        where = [jax.random.randint(jax.random.fold_in(key, axis), (), 0, length) for axis, length in enumerate(values.shape)]
        where[longest] = (where[longest] + shift) % values.shape[longest]
        spots.append(tuple(where))
    return values.at[spots[0]].set(least).at[spots[1]].set(high)


def shard_levels(key, shape, cuts, smallest, high):
    level = 1.0
    for position, parts in cuts:
        draws = jax.random.uniform(jax.random.fold_in(jax.random.fold_in(key, 6), position), (parts,), jnp.float32, smallest / len(cuts), high / len(cuts))
        level = level * jnp.repeat(jnp.exp(draws), shape[position] // parts).reshape((-1,) + (1,) * (len(shape) - 1 - position))
    return level


def split_up(count, total, limit, lean):
    weights = [(1 << 20) // math.isqrt(rank ** lean) + 1 for rank in range(2, count + 1)]
    spare, given = total - limit - (count - 1), [1] * (count - 1)
    while spare > 0:
        free = [i for i in range(count - 1) if given[i] < limit]
        whole, remaining = sum([weights[i] for i in free]), spare
        for i in free:
            addition = min(limit - given[i], max(1, remaining * weights[i] // whole), spare)
            given[i] = given[i] + addition
            spare = spare - addition
    return np.array([limit] + given)


def uneven(key, number_of, total, bound, skew):
    if number_of == 2:
        one = jax.random.randint(key, (), max(1, total - bound), min(bound, total - 1) + 1)
        return jnp.stack([one, total - one])
    lengths = jnp.asarray(split_up(number_of, total, bound, skew), jnp.int32)
    twos = (number_of - 1) // 2
    donor, sink = lengths[1:1 + 2 * twos:2], lengths[2:2 + 2 * twos:2]
    room = jnp.minimum(donor - 1, bound - sink)
    passed = jax.random.randint(jax.random.fold_in(key, 1), (twos,), 0, 1 << 20) % (room + 1)
    lengths = lengths.at[1:1 + 2 * twos:2].set(donor - passed).at[2:2 + 2 * twos:2].set(sink + passed)
    return lengths[jax.random.permutation(jax.random.fold_in(key, 2), number_of)]


def noise(rng, shape, scale, most, shards=(), kind=jnp.bfloat16):
    loudness = shard_levels(rng, shape, shards, -0.22, 0.18) if shards else 1.0
    result = jax.random.normal(rng, shape, jnp.float32) * scale * loudness
    return jnp.minimum(jnp.maximum(result, -most), most).astype(kind)


def setup_inputs(seed: int = 0) -> dict:
    key_list = jax.random.split(jax.random.key(seed), 12)
    return {
        "prompt_hidden": noise(key_list[0], (PROMPT, D), 1.0, 6.0, ((0, 16), (1, 16))),
        "kv_weight": noise(key_list[1], (D, 2 * KVH * HD), D ** -0.5, 0.046875, ((0, 16),)),
        "cache_k": draw_cache_k(jax.random.fold_in(key_list[11], 71), 0),
        "cache_v": noise(key_list[3], (CACHE, KVH * HD), 1.0, 6.0, ((0, 16),)),
        "prompt_q": draw_prompt_q(jax.random.fold_in(key_list[11], 71), 0),
        "dec_q": draw_dec_q(jax.random.fold_in(key_list[11], 71), 0),
        "dec_k": noise(key_list[6], (DEC, KVH * HD), 1.0, 6.0, ((0, 16),)),
        "dec_v": noise(key_list[7], (DEC, KVH * HD), 1.0, 6.0, ((0, 16),)),
        "cache_lengths": uneven(key_list[8], N_CTX, N_CTX * CACHE_DEV // 2, CACHE_DEV, 2).astype(jnp.int32),
        "prompt_pos": jax.random.permutation(key_list[9], PROMPT).astype(jnp.int32),
        "dec_owner": plant(jax.random.randint(key_list[10], (DEC,), 0, N_CTX), jax.random.fold_in(key_list[10], 1), 0, N_CTX - 1).astype(jnp.int32),
    }


NEG = -1.0e30


def rounded(weights):
    narrow = lax.optimization_barrier(weights.astype(jnp.bfloat16))
    return narrow.astype(jnp.float32)


def reference(prompt_hidden, kv_weight, cache_k, cache_v, prompt_q, dec_q, dec_k, dec_v, cache_lengths, prompt_pos, dec_owner):
    scale = HD ** -0.5
    group = H // KVH
    width = KVH * HD
    joined = jnp.dot(prompt_hidden, kv_weight, preferred_element_type=jnp.float32).astype(jnp.bfloat16)
    keys_all = jnp.concatenate([cache_k, joined[:, :width]], 0)
    values_all = jnp.concatenate([cache_v, joined[:, width:]], 0)
    key_heads = keys_all.reshape(CACHE + PROMPT, KVH, HD).transpose(1, 0, 2)
    value_heads = values_all.reshape(CACHE + PROMPT, KVH, HD).transpose(1, 0, 2)
    slots = jnp.arange(CACHE, dtype=jnp.int32)
    hosts = slots // CACHE_DEV
    valid = (slots % CACHE_DEV) < cache_lengths[hosts]
    block = math.gcd(PROMPT, 128)
    blocks = PROMPT // block
    query_heads = prompt_q.reshape(blocks, block, KVH, group, HD).transpose(2, 0, 1, 3, 4)
    pos_blocks = prompt_pos.reshape(blocks, block)

    def prefill_head(item):
        queries, keys, values = item
        keys_wide = keys.astype(jnp.float32)
        values_wide = values.astype(jnp.float32)

        def one_block(inner):
            query_block, positions = inner
            causal = prompt_pos[None, :] <= positions[:, None]
            mask = jnp.concatenate([jnp.broadcast_to(valid[None, :], (block, CACHE)), causal], 1)
            scores = jnp.einsum("rgd,nd->grn", query_block.astype(jnp.float32), keys_wide) * scale
            scores = jnp.where(mask[None], scores, NEG)
            top = jnp.max(scores, axis=-1, keepdims=True)
            weights = jnp.where(mask[None], jnp.exp(scores - top), 0.0)
            total = jnp.sum(weights, axis=-1)
            summed = jnp.einsum("grn,nd->rgd", rounded(weights), values_wide)
            return summed / total.T[:, :, None]

        return lax.map(one_block, (queries, pos_blocks))

    prompt_out = lax.map(prefill_head, (query_heads, key_heads, value_heads))
    prompt_out = prompt_out.transpose(1, 2, 0, 3, 4).reshape(PROMPT, H * HD).astype(jnp.bfloat16)

    dec_heads = dec_q.reshape(DEC, KVH, group, HD).transpose(1, 0, 2, 3)
    own_keys = dec_k.reshape(DEC, KVH, HD).transpose(1, 0, 2)
    own_values = dec_v.reshape(DEC, KVH, HD).transpose(1, 0, 2)
    dec_mask = valid[None, :] & (hosts[None, :] <= dec_owner[:, None])

    def decode_head(item):
        queries, keys, values, own_key, own_value = item
        queries_wide = queries.astype(jnp.float32)
        scores = jnp.einsum("rgd,nd->grn", queries_wide, keys.astype(jnp.float32)) * scale
        scores = jnp.where(dec_mask[None], scores, NEG)
        own = jnp.einsum("rgd,rd->gr", queries_wide, own_key.astype(jnp.float32)) * scale
        top = jnp.maximum(jnp.max(scores, axis=-1), own)
        weights = jnp.where(dec_mask[None], jnp.exp(scores - top[..., None]), 0.0)
        own_weight = jnp.exp(own - top)
        summed = jnp.einsum("grn,nd->rgd", rounded(weights), values.astype(jnp.float32))
        summed = summed + rounded(own_weight).T[:, :, None] * own_value.astype(jnp.float32)[:, None, :]
        total = jnp.sum(weights, axis=-1) + own_weight
        return summed / total.T[:, :, None]

    dec_out = lax.map(decode_head, (dec_heads, key_heads[:, :CACHE], value_heads[:, :CACHE], own_keys, own_values))
    dec_out = dec_out.transpose(1, 0, 2, 3).reshape(DEC, H * HD).astype(jnp.bfloat16)
    return prompt_out, dec_out
```

```python
import functools
import math

import jax
import jax.numpy as jnp
from jax import lax
from jax.experimental import pallas as pl
from jax.experimental.pallas import tpu as pltpu
from jax.sharding import PartitionSpec as P

HD = 128
HEADS = 8
ROWS = 64
DROWS = 8
PR = HEADS * ROWS
QR = PR + HEADS * DROWS
MSG = QR + 16
SLOTS = 1024
CHUNK = 256
EXP = HD ** -0.5 * math.log2(math.e)
MASKED = -1e30
FLOOR = -1e20
BASE = 32
F32 = jnp.float32
BF16 = jnp.bfloat16


def swap(f):
    out = []
    for i in range(256):
        y, xh, core, xl, z = i // 64, i // 32 % 2, i // 16 % 2, i // 8 % 2, i % 8
        y, xh, core, xl, z = f(y, xh, core, xl, z)
        out.append((i, (((y * 2 + xh) * 2 + core) * 2 + xl) * 8 + z))
    return out


CORE = swap(lambda y, xh, c, xl, z: (y, xh, 1 - c, xl, z))
XADJ = swap(lambda y, xh, c, xl, z: (y, 1 - xh, c, 1 - xl, z))
XFAR = swap(lambda y, xh, c, xl, z: (y, 1 - xh, c, xl, z))
XLOW = swap(lambda y, xh, c, xl, z: (y, xh, c, 1 - xl, z))
Y1, Y2, Y3 = (swap(lambda y, xh, c, xl, z, k=k: (y ^ k, xh, c, xl, z)) for k in (1, 2, 3))
Z1, Z2, Z6 = (swap(lambda y, xh, c, xl, z, k=k: (y, xh, c, xl, z ^ k)) for k in (1, 2, 6))


def move(x, pairs):
    return lax.ppermute(x, ("ctx", "tp"), pairs)


def vmem(mib):
    return pltpu.CompilerParams(vmem_limit_bytes=mib * 1024 * 1024)


def project_kernel(ids, hid, ks, vs, kk, vk, send, keep):
    h = hid[...]
    send[0, :, :HD] = jnp.dot(h, ks[...], preferred_element_type=F32).astype(BF16)
    send[0, :, HD:] = jnp.dot(h, vs[...], preferred_element_type=F32).astype(BF16)
    keep[0, :, :HD] = jnp.dot(h, kk[...], preferred_element_type=F32)
    keep[0, :, HD:] = jnp.dot(h, vk[...], preferred_element_type=F32)


def project(ids, hidden, weight):
    feats = hidden.shape[1]
    def col(shift, flip):
        def index(i, ids):
            side = 1 - ids[1] if flip else ids[1]
            return (0, shift + side * 4 + i)
        return pl.BlockSpec((feats, HD), index)
    out = pl.BlockSpec((1, ROWS, 2 * HD), lambda i, ids: (i, 0, 0))
    return pl.pallas_call(
        project_kernel,
        grid_spec=pltpu.PrefetchScalarGridSpec(
            num_scalar_prefetch=1,
            grid=(4,),
            in_specs=[
                pl.BlockSpec((ROWS, feats), lambda i, ids: (0, 0)),
                col(0, True), col(8, True), col(0, False), col(8, False),
            ],
            out_specs=[out, out],
        ),
        out_shape=[
            jax.ShapeDtypeStruct((4, ROWS, 2 * HD), BF16),
            jax.ShapeDtypeStruct((4, ROWS, 2 * HD), F32),
        ],
        compiler_params=vmem(32),
        name="project",
    )(ids, hidden, weight, weight, weight, weight)


def pack_kv_kernel(ids, lengths, k, v, k_other, v_other, own, give):
    n = lengths[0]
    row = lax.broadcasted_iota(jnp.int32, (16, HD), 0)
    value = jnp.where(row < 8, n // BASE, n % BASE).astype(F32).astype(BF16)
    for out, keys, vals in ((own, k, v), (give, k_other, v_other)):
        out[0:SLOTS, :] = keys[...]
        out[SLOTS:2 * SLOTS, :] = vals[...]
        out[2 * SLOTS:2 * SLOTS + 16, :] = value


def pack_kv(ids, lengths, cache_k, cache_v):
    own = pl.BlockSpec((SLOTS, HD), lambda i, ids, lengths: (0, ids[0]))
    other = pl.BlockSpec((SLOTS, HD), lambda i, ids, lengths: (0, ids[0] ^ 4))
    out = pl.BlockSpec((2 * SLOTS + 16, HD), lambda i, ids, lengths: (0, 0))
    return pl.pallas_call(
        pack_kv_kernel,
        grid_spec=pltpu.PrefetchScalarGridSpec(
            num_scalar_prefetch=2,
            grid=(1,),
            in_specs=[own, own, other, other],
            out_specs=[out, out],
        ),
        out_shape=[jax.ShapeDtypeStruct((2 * SLOTS + 16, HD), BF16)] * 2,
        compiler_params=vmem(16),
        name="pack_kv",
    )(ids, lengths, cache_k, cache_v, cache_k, cache_v)


def pack_q_kernel(owner, pq, dq, out):
    for j in range(HEADS):
        out[j * ROWS:(j + 1) * ROWS, :] = pq[:, j * HD:(j + 1) * HD]
    d = dq[...].astype(F32)
    rows = jnp.concatenate([d[:, j * HD:(j + 1) * HD] for j in range(HEADS)], 0)
    out[PR:QR, :] = rows.astype(BF16)
    row = lax.broadcasted_iota(jnp.int32, (16, HD), 0)
    who = jnp.zeros((16, HD), jnp.int32)
    for r in range(DROWS):
        who = jnp.where(row == r, owner[r], who)
    out[QR:MSG, :] = who.astype(F32).astype(BF16)


def pack_q(owner, prompt_q, dec_q):
    return pl.pallas_call(
        pack_q_kernel,
        in_specs=[
            pl.BlockSpec(memory_space=pltpu.SMEM),
            pl.BlockSpec(memory_space=pltpu.VMEM),
            pl.BlockSpec(memory_space=pltpu.VMEM),
        ],
        out_specs=pl.BlockSpec(memory_space=pltpu.VMEM),
        out_shape=jax.ShapeDtypeStruct((MSG, HD), BF16),
        compiler_params=vmem(16),
        name="pack_q",
    )(owner, prompt_q, dec_q)


BLOCKS = ((0, 256), (256, 256), (512, 64))


def cache_kernel(hosts, q, kv0, kv1, kv2, kv3, out, acc, top):
    acc[...] = jnp.zeros_like(acc)
    top[...] = jnp.full_like(top, FLOOR)
    owner = q[QR:MSG, :].astype(F32)[:DROWS]
    owner = jnp.concatenate([owner] * HEADS, 0)
    ones = jnp.ones((CHUNK, HD), BF16)
    for n, kv in enumerate((kv0, kv1, kv2, kv3)):
        tail = kv[2 * SLOTS:2 * SLOTS + 16, :].astype(F32)
        length = jnp.max(tail[:8] * BASE + tail[8:]).astype(jnp.int32)
        seen = owner >= hosts[n].astype(F32)
        seen = jnp.concatenate([seen.astype(F32)] * (CHUNK // HD), 1) > 0.5

        def step(c, carry, kv=kv, length=length, seen=seen):
            k = kv[pl.ds(pl.multiple_of(c * CHUNK, CHUNK), CHUNK), :]
            v = kv[pl.ds(pl.multiple_of(SLOTS + c * CHUNK, CHUNK), CHUNK), :]
            v = jnp.concatenate([v, ones], 1)
            left = length - c * CHUNK
            for start, size in BLOCKS:
                rows = slice(start, start + size)
                s = lax.dot_general(q[rows, :], k, (((1,), (1,)), ((), ())), preferred_element_type=F32)
                ok = lax.broadcasted_iota(jnp.int32, (size, CHUNK), 1) < left
                if start == PR:
                    ok = ok & seen
                s = jnp.where(ok, s, MASKED)
                old = top[rows, :]
                new = jnp.maximum(old, jnp.max(s, axis=1, keepdims=True))
                p = jnp.exp2((s - jnp.concatenate([new] * (CHUNK // HD), 1)) * EXP)
                shrink = jnp.exp2((old - new) * EXP)
                acc[rows, :] = acc[rows, :] * jnp.concatenate([shrink, shrink], 1) + jnp.dot(
                    p.astype(BF16), v, preferred_element_type=F32
                )
                top[rows, :] = new
            return carry

        lax.fori_loop(0, (length + CHUNK - 1) // CHUNK, step, 0)
    total = acc[:, HD:]
    some = total > 0.0
    total = jnp.where(some, total, 1.0)
    out[0:QR, :] = jnp.where(some, acc[:, :HD] / total, 0.0).astype(BF16)
    top[...] = jnp.where(some, top[...] * EXP + jnp.log2(total), FLOOR)
    diagonal = lax.broadcasted_iota(jnp.int32, (HD, HD), 0) == lax.broadcasted_iota(jnp.int32, (HD, HD), 1)
    index = lax.broadcasted_iota(jnp.int32, (16, HD), 0)
    packed = jnp.zeros((16, HD), F32)
    for b in range(5):
        if b < 4:
            block = top[b * HD:(b + 1) * HD, :]
        else:
            block = jnp.concatenate([top[PR:QR, :], jnp.zeros((HD - QR + PR, HD), F32)], 0)
        line = jnp.sum(jnp.where(diagonal, block, 0.0), axis=0, keepdims=True)
        for i in range(3):
            piece = line.astype(BF16).astype(F32)
            packed = jnp.where(index == 3 * b + i, piece, packed)
            line = line - piece
    out[QR:MSG, :] = packed.astype(BF16)


def cache_attend(hosts, q, kvs):
    whole = pl.BlockSpec(memory_space=pltpu.VMEM)
    return pl.pallas_call(
        cache_kernel,
        in_specs=[pl.BlockSpec(memory_space=pltpu.SMEM)] + [whole] * 5,
        out_specs=whole,
        out_shape=jax.ShapeDtypeStruct((MSG, HD), BF16),
        scratch_shapes=[pltpu.VMEM((QR, 2 * HD), F32), pltpu.VMEM((QR, HD), F32)],
        compiler_params=vmem(32),
        cost_estimate=pl.CostEstimate(flops=4 * QR * 2048 * HD, bytes_accessed=5 << 20, transcendentals=QR * 2048),
        name="cache_attend",
    )(hosts, q, *kvs)


def final_kernel(ids, q, m0, m1, m2, m3, pa, pb, pos, dk, dv, out_p, out_d, keys, vals):
    parts = (m0, m1, m2, m3)
    vals[:, HD:] = jnp.ones((1024, HD), BF16)
    lines = []
    lane = lax.broadcasted_iota(jnp.int32, (1, HD), 1)
    for n, ref in enumerate((pa, pb)):
        for i in range(8):
            at = (n * 8 + i) * ROWS
            keys[at:at + ROWS, :] = ref[i, 0:ROWS, 0:HD]
            vals[at:at + ROWS, 0:HD] = ref[i, 0:ROWS, HD:2 * HD]
            tail = ref[i, ROWS:ROWS + 16, 0:HD].astype(F32)
            lines.append(tail[0:1] * BASE + tail[1:2])
    where = jnp.concatenate(
        [jnp.where(lane < ROWS, lines[2 * i], lines[2 * i + 1]) for i in range(8)], 1
    )
    diagonal = lax.broadcasted_iota(jnp.int32, (HD, HD), 0) == lax.broadcasted_iota(jnp.int32, (HD, HD), 1)

    def column(ref, b):
        tail = ref[QR:MSG, :].astype(F32)
        line = tail[3 * b:3 * b + 1] + tail[3 * b + 1:3 * b + 2] + tail[3 * b + 2:3 * b + 3]
        return jnp.sum(jnp.where(diagonal, line, 0.0), axis=1, keepdims=True)

    def merge(b, rows, size, level, value):
        levels = [column(ref, b)[:size] for ref in parts]
        high = level
        for x in levels:
            high = jnp.maximum(high, x)
        weight = jnp.exp2(level - high)
        summed, total = weight * value, weight
        for x, ref in zip(levels, parts):
            weight = jnp.exp2(x - high)
            summed = summed + weight * ref[rows, :].astype(F32)
            total = total + weight
        return summed / total

    mine = jnp.concatenate([pos[...], pos[...]], 0)[:, 0:1]
    mask = where <= mine
    for b in range(4):
        rows = slice(b * HD, (b + 1) * HD)
        s = lax.dot_general(q[rows, :], keys[...], (((1,), (1,)), ((), ())), preferred_element_type=F32)
        s = jnp.where(mask, s, MASKED)
        high = jnp.max(s, axis=1, keepdims=True)
        p = jnp.exp2((s - high) * EXP)
        o = jnp.dot(p.astype(BF16), vals[...], preferred_element_type=F32)
        total = o[:, HD:HD + 1]
        merged = merge(b, rows, HD, high * EXP + jnp.log2(total), o[:, :HD] / total).astype(BF16)
        out_p[:, 2 * b * HD:(2 * b + 1) * HD] = merged[:ROWS]
        out_p[:, (2 * b + 1) * HD:(2 * b + 2) * HD] = merged[ROWS:]
    rows = slice(PR, QR)
    key = jnp.concatenate([dk[...].astype(F32)] * HEADS, 0)
    value = jnp.concatenate([dv[...].astype(F32)] * HEADS, 0)
    level = jnp.sum(q[rows, :].astype(F32) * key, axis=1, keepdims=True) * EXP
    merged = merge(4, rows, QR - PR, level, value)
    for j in range(HEADS):
        out_d[:, j * HD:(j + 1) * HD] = merged[j * DROWS:(j + 1) * DROWS].astype(BF16)


def final(ids, q, parts, pa, pb, pos, dec_k, dec_v):
    whole = pl.BlockSpec(memory_space=pltpu.VMEM)
    own = pl.BlockSpec((DROWS, HD), lambda i, ids: (0, ids[0]))
    def full(shape):
        return pl.BlockSpec(shape, lambda i, ids: (0,) * len(shape))
    return pl.pallas_call(
        final_kernel,
        grid_spec=pltpu.PrefetchScalarGridSpec(
            num_scalar_prefetch=1,
            grid=(1,),
            in_specs=[full((MSG, HD))] * 5
            + [full((8, ROWS + 16, 2 * HD))] * 2
            + [full((ROWS, HD)), own, own],
            out_specs=[full((ROWS, HEADS * HD)), full((DROWS, HEADS * HD))],
            scratch_shapes=[pltpu.VMEM((1024, HD), BF16), pltpu.VMEM((1024, 2 * HD), BF16)],
        ),
        out_shape=[
            jax.ShapeDtypeStruct((ROWS, HEADS * HD), BF16),
            jax.ShapeDtypeStruct((DROWS, HEADS * HD), BF16),
        ],
        compiler_params=vmem(32),
        name="final",
    )(ids, q, *parts, pa, pb, pos, dec_k, dec_v)


def body(
    prompt_hidden, kv_weight, cache_k, cache_v, prompt_q, dec_q, dec_k, dec_v,
    cache_lengths, prompt_pos, dec_owner,
):
    host = lax.axis_index("ctx")
    tp = lax.axis_index("tp")
    xl, z = tp // 8, tp % 8
    ids = jnp.stack([tp // 2, xl])
    hosts = jnp.stack([host, host ^ 1, host ^ 2, host ^ 3])

    send, keep = project(ids, prompt_hidden, kv_weight)
    got = move(send, XLOW)

    kv_own, kv_give = pack_kv(ids, cache_lengths, cache_k, cache_v)
    kv_adj = move(kv_give, XADJ)
    kv_core = move(kv_own, CORE)
    kv_diag = move(kv_adj, CORE)
    q_own = pack_q(dec_owner, prompt_q, dec_q)
    qs = [q_own, move(q_own, Y1), move(q_own, Y2), move(q_own, Y3)]

    def halve(total, bit):
        both = total.reshape((2, total.shape[0] // 2) + total.shape[1:])
        pick = functools.partial(lax.dynamic_index_in_dim, both, axis=0, keepdims=False)
        return pick(1 - bit).astype(BF16), pick(bit)

    send, keep = halve(keep + got.astype(F32), z // 4)
    got = move(send, Z6)
    send, keep = halve(keep + got.astype(F32), z // 2 % 2)
    got = move(send, Z2)
    total = (keep + got.astype(F32))[0]
    got = move(total.astype(BF16), Z1)
    joined = (total + got.astype(F32)).astype(BF16)

    where = jnp.stack([prompt_pos // BASE, prompt_pos % BASE]).astype(F32).astype(BF16)
    where = jnp.pad(jnp.tile(where, (1, 4)), ((0, 14), (0, 0)))
    piece = jnp.concatenate([joined, where], 0)
    pair = jnp.stack([piece, move(piece, XFAR)])
    quarter = jnp.concatenate([pair, move(pair, Y1), move(pair, Y2), move(pair, Y3)], 0)
    other = move(quarter, CORE)

    kvs = [kv_own, kv_core, kv_adj, kv_diag]
    back = [cache_attend(hosts, q, kvs) for q in qs]
    parts = [back[0], move(back[1], Y1), move(back[2], Y2), move(back[3], Y3)]
    pos = jnp.broadcast_to(prompt_pos.astype(F32)[:, None], (ROWS, HD))
    return tuple(final(ids, q_own, parts, quarter, other, pos, dec_k, dec_v))


def solution(mesh):
    in_specs = (
        P("ctx", "tp"), P("tp", None), P("ctx", None), P("ctx", None), P("ctx", "tp"),
        P("ctx", "tp"), P("ctx", None), P("ctx", None), P("ctx"), P("ctx"), P("ctx"),
    )
    out_specs = (P("ctx", "tp"), P("ctx", "tp"))
    return jax.shard_map(body, mesh=mesh, in_specs=in_specs, out_specs=out_specs, check_vma=False)
```

```python
import functools
import math

import jax
import jax.numpy as jnp
from jax import lax
from jax.experimental import pallas as pl
from jax.experimental.pallas import tpu as pltpu
from jax.sharding import PartitionSpec as P

HD = 128
HEADS = 8
KVH = 8
ROWS = 64
DROWS = 8
PR = HEADS * ROWS
QR = PR + HEADS * DROWS
MSG = QR + 16
SLOTS = 1024
CHUNK = 256
EXP = HD ** -0.5 * math.log2(math.e)
MASKED = -1e30
FLOOR = -1e20
BASE = 32
F32 = jnp.float32
BF16 = jnp.bfloat16


def swap(f):
    out = []
    for i in range(256):
        y, xh, core, xl, z = i // 64, i // 32 % 2, i // 16 % 2, i // 8 % 2, i % 8
        y, xh, core, xl, z = f(y, xh, core, xl, z)
        out.append((i, (((y * 2 + xh) * 2 + core) * 2 + xl) * 8 + z))
    return out


CORE = swap(lambda y, xh, c, xl, z: (y, xh, 1 - c, xl, z))
XADJ = swap(lambda y, xh, c, xl, z: (y, 1 - xh, c, 1 - xl, z))
XFAR = swap(lambda y, xh, c, xl, z: (y, 1 - xh, c, xl, z))
XLOW = swap(lambda y, xh, c, xl, z: (y, xh, c, 1 - xl, z))
Y1, Y2, Y3 = (swap(lambda y, xh, c, xl, z, k=k: (y ^ k, xh, c, xl, z)) for k in (1, 2, 3))
Z1, Z2, Z6 = (swap(lambda y, xh, c, xl, z, k=k: (y, xh, c, xl, z ^ k)) for k in (1, 2, 6))


def tie(x, *others):
    return lax.optimization_barrier((x, *others))[0]


def move(x, pairs):
    return lax.ppermute(x, ("ctx", "tp"), pairs)


def vmem(mib):
    return pltpu.CompilerParams(vmem_limit_bytes=mib * 1024 * 1024)


PARTS = 4
KV = 2 * SLOTS + 16
PIECE = 2 * ROWS + 16
PAIR = 2 * PIECE


def project_kernel(tp, hidden, weight, send, keep, h, w, acc, sem_w, sem_h):
    side = tp[0] // 8
    deep = hidden.shape[1] // PARTS
    copy = pltpu.make_async_copy
    copy_h = copy(hidden, h, sem_h)
    copies = [
        copy(weight.at[pl.ds(i * deep, deep)], w.at[pl.ds(i * deep, deep)], sem_w.at[i]) for i in range(PARTS)
    ]
    copy_h.start()
    for x in copies:
        x.start()
    copy_h.wait()
    for i in range(PARTS):
        copies[i].wait()
        part = slice(i * deep, (i + 1) * deep)
        product = jnp.dot(h[:, part], w[part, :], preferred_element_type=F32)
        acc[...] = product if i == 0 else acc[...] + product
    for i in range(4):
        for out, where in ((send, 1 - side), (keep, side)):
            at = (where * 4 + i) * HD
            for v in range(2):
                block = acc[:, pl.ds(pl.multiple_of(at + v * KVH * HD, HD), HD)]
                out[i, v * ROWS:(v + 1) * ROWS, :] = block.astype(out.dtype)


def far_call(kernel, scalars, arrays, outs, scratch, name):
    whole = pl.BlockSpec(memory_space=pltpu.VMEM)
    return pl.pallas_call(
        kernel,
        in_specs=[pl.BlockSpec(memory_space=pltpu.SMEM)] * len(scalars)
        + [pl.BlockSpec(memory_space=pl.ANY)] * len(arrays),
        out_specs=[whole] * len(outs),
        out_shape=[jax.ShapeDtypeStruct(shape, dtype) for shape, dtype in outs],
        scratch_shapes=scratch,
        compiler_params=vmem(12),
        name=name,
    )(*scalars, *[pltpu.with_memory_space_constraint(x, pltpu.HBM) for x in arrays])


def project(tp, hidden, weight):
    feats, width = weight.shape
    half = (4, 2 * ROWS, HD)
    scratch = [
        pltpu.VMEM((ROWS, feats), BF16),
        pltpu.VMEM((feats, width), BF16),
        pltpu.VMEM((ROWS, width), F32),
        pltpu.SemaphoreType.DMA((PARTS,)),
        pltpu.SemaphoreType.DMA,
    ]
    return far_call(project_kernel, (tp,), (hidden, weight), [(half, BF16), (half, F32)], scratch, "project")


def pack_kernel(
    tp, lengths, owner, pos, cache_k, cache_v, prompt_q, dec_q, dec_k, dec_v,
    kv_own, kv_give, q_own, own_kv, pos_line, pos_column,
    c, pq, dq, dkv, owner_s, pos_s, sem_c, sem_s,
):
    head = tp[0] // 2
    own = pl.ds(pl.multiple_of(head * HD, HD), HD)
    other = pl.ds(pl.multiple_of((head ^ 4) * HD, HD), HD)
    copy = pltpu.make_async_copy
    copies = [
        copy(source, target, sem_s.at[i])
        for i, (source, target) in enumerate((
            (owner, owner_s), (pos, pos_s), (prompt_q, pq), (dec_q, dq),
            (dec_k.at[:, own], dkv.at[0]), (dec_v.at[:, own], dkv.at[1]),
        ))
    ]
    copies_c = [
        copy(source.at[:, part], c.at[i], sem_c.at[i])
        for i, (source, part) in enumerate(
            ((cache_k, other), (cache_v, other), (cache_k, own), (cache_v, own))
        )
    ]
    for x in copies + copies_c:
        x.start()
    for x in copies:
        x.wait()
    for j in range(HEADS):
        q_own[j * ROWS:(j + 1) * ROWS, :] = pq[:, j * HD:(j + 1) * HD]
    d = dq[...].astype(F32)
    rows = jnp.concatenate([d[:, j * HD:(j + 1) * HD] for j in range(HEADS)], 0)
    q_own[PR:QR, :] = rows.astype(BF16)
    row = lax.broadcasted_iota(jnp.int32, (16, HD), 0)
    who = jnp.zeros((16, HD), jnp.int32)
    for r in range(DROWS):
        who = jnp.where(row == r, owner_s[r], who)
    q_own[QR:MSG, :] = who.astype(F32).astype(BF16)
    lane = lax.broadcasted_iota(jnp.int32, (16, HD), 1) % ROWS
    eight = lax.broadcasted_iota(jnp.int32, (DROWS, HD), 0)
    line = jnp.zeros((16, HD), jnp.int32)
    for b in range(ROWS // DROWS):
        column = jnp.zeros((DROWS, HD), jnp.int32)
        for r in range(DROWS):
            column = jnp.where(eight == r, pos_s[b * DROWS + r], column)
            line = jnp.where(lane == b * DROWS + r, pos_s[b * DROWS + r], line)
        pos_column[b * DROWS:(b + 1) * DROWS, :] = column.astype(F32)
    line = jnp.where(row == 0, line // BASE, jnp.where(row == 1, line % BASE, 0))
    pos_line[...] = line.astype(F32).astype(BF16)
    own_kv[0:DROWS, :] = dkv[0].astype(F32)
    own_kv[DROWS:2 * DROWS, :] = dkv[1].astype(F32)

    n = lengths[0]
    value = jnp.where(row < 8, n // BASE, n % BASE).astype(F32).astype(BF16)
    filled = lax.broadcasted_iota(jnp.int32, (SLOTS, HD), 0) < n
    for i, out in enumerate((kv_give, kv_own)):
        copies_c[2 * i].wait()
        copies_c[2 * i + 1].wait()
        keys = c[2 * i].astype(F32)
        out[0:SLOTS, :] = jnp.where(filled, keys, keys[0:1]).astype(BF16)
        out[SLOTS:2 * SLOTS, :] = jnp.where(filled, c[2 * i + 1].astype(F32), 0.0).astype(BF16)
        out[2 * SLOTS:KV, :] = value


def pack(tp, lengths, *arrays):
    outs = [((KV, HD), BF16), ((KV, HD), BF16), ((MSG, HD), BF16), ((2 * DROWS, HD), F32), ((16, HD), BF16), ((ROWS, HD), F32)]
    scratch = [
        pltpu.VMEM((4, SLOTS, HD), BF16),
        pltpu.VMEM((ROWS, HEADS * HD), BF16),
        pltpu.VMEM((DROWS, HEADS * HD), BF16),
        pltpu.VMEM((2, DROWS, HD), BF16),
        pltpu.SMEM((DROWS,), jnp.int32),
        pltpu.SMEM((ROWS,), jnp.int32),
        pltpu.SemaphoreType.DMA((4,)),
        pltpu.SemaphoreType.DMA((6,)),
    ]
    return far_call(pack_kernel, (tp, lengths), arrays, outs, scratch, "pack")


def glue(kernel, scalars, arrays, outs, name):
    whole = pl.BlockSpec(memory_space=pltpu.VMEM)
    return pl.pallas_call(
        kernel,
        in_specs=[pl.BlockSpec(memory_space=pltpu.SMEM)] * len(scalars) + [whole] * len(arrays),
        out_specs=[whole] * len(outs),
        out_shape=[jax.ShapeDtypeStruct(shape, dtype) for shape, dtype in outs],
        compiler_params=vmem(4),
        name=name,
    )(*scalars, *arrays)


def halve_kernel(bit, tp, keep, got, send, left):
    half = send.shape[0]
    mine = tp[0] // bit % 2
    for i in range(half):
        j = (1 - mine) * half + i
        send[i] = (keep[j] + got[j].astype(F32)).astype(BF16)
        j = mine * half + i
        left[i] = keep[j] + got[j].astype(F32)


def halve(bit, tp, keep, got):
    shape = (keep.shape[0] // 2,) + keep.shape[1:]
    return glue(functools.partial(halve_kernel, bit), (tp,), (keep, got), ((shape, BF16), (shape, F32)), "halve")


def add_kernel(keep, got, send, total):
    x = keep[0] + got[0].astype(F32)
    send[...] = x.astype(BF16)
    total[...] = x


def join_kernel(total, got, line, piece):
    piece[0:2 * ROWS, :] = (total[...] + got[...].astype(F32)).astype(BF16)
    piece[2 * ROWS:PIECE, :] = line[...]


def letters_kernel(piece, got, back1, back2, back3, out1, out2, out3):
    for back, out in ((back1, out1), (back2, out2), (back3, out3)):
        out[0:PIECE, :] = piece[...]
        out[PIECE:PAIR, :] = got[...]
        out[PAIR:PAIR + MSG, :] = back[...]


def near_kernel(piece, got, m1, m2, m3, out):
    out[0:PIECE, :] = piece[...]
    out[PIECE:PAIR, :] = got[...]
    for i, m in enumerate((m1, m2, m3)):
        out[(i + 1) * PAIR:(i + 2) * PAIR, :] = m[0:PAIR, :]


BLOCK = 192


def absorb(ctx, n, kv, qs, acc, top):
    tail = kv[2 * SLOTS:2 * SLOTS + 16, :].astype(F32)
    length = jnp.max(tail[:8] * BASE + tail[8:]).astype(jnp.int32)
    host = (ctx[0] ^ n).astype(F32)

    def chunk(base, size):
        k = kv[pl.ds(pl.multiple_of(base, 256), size), :]
        v = kv[pl.ds(pl.multiple_of(SLOTS + base, 256), size), :]
        one = lax.broadcasted_iota(jnp.int32, (size, HD), 0) < length - base
        v = jnp.concatenate([v, jnp.where(one, 1.0, 0.0).astype(BF16)], 1)
        for g, q in enumerate(qs):
            for start in range(0, QR, BLOCK):
                rows = slice(g * QR + start, g * QR + start + BLOCK)
                s = lax.dot_general(
                    q[start:start + BLOCK, :], k, (((1,), (1,)), ((), ())), preferred_element_type=F32
                )
                old = top[rows, :]
                new = jnp.maximum(old, jnp.max(s, axis=1, keepdims=True))
                less = new
                if start + BLOCK > PR:
                    owner = q[QR:MSG, :].astype(F32)[:DROWS]
                    owner = jnp.concatenate([jnp.full((BLOCK - QR + PR, HD), 99.0)] + [owner] * HEADS, 0)
                    seen = owner >= host
                    new = jnp.where(seen, new, old)
                    less = jnp.where(seen, new, -MASKED)
                p = jnp.exp2((s - jnp.concatenate([less] * (size // HD), 1)) * EXP)
                shrink = jnp.exp2((old - new) * EXP)
                acc[rows, :] = acc[rows, :] * jnp.concatenate([shrink, shrink], 1) + jnp.dot(
                    p.astype(BF16), v, preferred_element_type=F32
                )
                top[rows, :] = new

    rest = length % 512
    full = length // 512 + (rest > 256).astype(jnp.int32)

    def step(c, carry):
        chunk(c * 512, 512)
        return carry

    lax.fori_loop(0, full, step, 0)

    @pl.when((rest > 0) & (rest <= 256))
    def _():
        chunk(full * 512, 256)


def first_kernel(ctx, q0, q1, kv0, kv1, acc, top):
    acc[...] = jnp.zeros_like(acc)
    top[...] = jnp.full_like(top, FLOOR)
    for n, kv in enumerate((kv0, kv1)):
        absorb(ctx, n, kv, (q0, q1), acc, top)


def second_kernel(ctx, q0, q1, kv2, kv3, acc0, top0, out0, out1, acc, top):
    acc[...] = acc0[...]
    top[...] = top0[...]
    for n, kv in enumerate((kv2, kv3)):
        absorb(ctx, n + 2, kv, (q0, q1), acc, top)
    diagonal = lax.broadcasted_iota(jnp.int32, (HD, HD), 0) == lax.broadcasted_iota(jnp.int32, (HD, HD), 1)
    index = lax.broadcasted_iota(jnp.int32, (16, HD), 0)
    for g, out in enumerate((out0, out1)):
        rows = slice(g * QR, (g + 1) * QR)
        total = acc[rows, HD:]
        some = total > 0.0
        total = jnp.where(some, total, 1.0)
        out[0:QR, :] = jnp.where(some, acc[rows, :HD] / total, 0.0).astype(BF16)
        level = jnp.where(some, top[rows, :] * EXP + jnp.log2(total), FLOOR)
        packed = jnp.zeros((16, HD), F32)
        for b in range(5):
            block = level[b * HD:(b + 1) * HD, :]
            if b == 4:
                block = jnp.concatenate([block, jnp.zeros((HD - QR + PR, HD), F32)], 0)
            line = jnp.sum(jnp.where(diagonal, block, 0.0), axis=0, keepdims=True)
            for i in range(3):
                piece = line.astype(BF16).astype(F32)
                packed = jnp.where(index == 3 * b + i, piece, packed)
                line = line - piece
        out[QR:MSG, :] = packed.astype(BF16)


STATE = ((2 * QR, 2 * HD), (2 * QR, HD))


def cache_call(kernel, host, arrays, outs, scratch, name):
    whole = pl.BlockSpec(memory_space=pltpu.VMEM)
    return pl.pallas_call(
        kernel,
        in_specs=[pl.BlockSpec(memory_space=pltpu.SMEM)] + [whole] * len(arrays),
        out_specs=[whole] * len(outs),
        out_shape=[jax.ShapeDtypeStruct(shape, dtype) for shape, dtype in outs],
        scratch_shapes=[pltpu.VMEM(shape, F32) for shape in scratch],
        compiler_params=vmem(8),
        name=name,
    )(host, *arrays)


def cache_first(host, qs, kvs):
    return cache_call(first_kernel, host, (*qs, *kvs), [(x, F32) for x in STATE], (), "cache_first")


def cache_second(host, qs, kvs, state):
    return cache_call(
        second_kernel, host, (*qs, *kvs, *state), [((MSG, HD), BF16)] * 2, STATE, "cache_second"
    )


NEAR = 8


def lay_out(ref, keys, vals):
    vals[:, HD:] = jnp.ones((NEAR * ROWS, HD), BF16)
    lane = lax.broadcasted_iota(jnp.int32, (1, HD), 1)
    lines = []
    for i in range(NEAR):
        at = i * ROWS
        base = i * PIECE
        keys[at:at + ROWS, :] = ref[base:base + ROWS, :]
        vals[at:at + ROWS, 0:HD] = ref[base + ROWS:base + 2 * ROWS, :]
        tail = ref[base + 2 * ROWS:base + PIECE, :].astype(F32)
        lines.append(tail[0:1] * BASE + tail[1:2])
    return jnp.concatenate(
        [jnp.where(lane < ROWS, lines[2 * i], lines[2 * i + 1]) for i in range(NEAR // 2)], 1
    )


def prompt_part(q, mask, keys, vals):
    s = lax.dot_general(q, keys[...], (((1,), (1,)), ((), ())), preferred_element_type=F32)
    s = jnp.where(mask, s, MASKED)
    high = jnp.maximum(jnp.max(s, axis=1, keepdims=True), FLOOR)
    p = jnp.exp2((s - high) * EXP)
    o = jnp.dot(p.astype(BF16), vals[...], preferred_element_type=F32)
    return high * EXP, o[:, HD:], o[:, :HD]


def middle_kernel(q, m0, m1, m2, m3, near, own_kv, pos, out_d, value, level, keys, vals):
    parts = ((m0, 0), (m1, PAIR), (m2, PAIR), (m3, PAIR))
    where = lay_out(near, keys, vals)
    diagonal = lax.broadcasted_iota(jnp.int32, (HD, HD), 0) == lax.broadcasted_iota(jnp.int32, (HD, HD), 1)

    def column(ref, base, b):
        tail = ref[base + QR:base + MSG, :].astype(F32)
        line = tail[3 * b:3 * b + 1] + tail[3 * b + 1:3 * b + 2] + tail[3 * b + 2:3 * b + 3]
        return jnp.sum(jnp.where(diagonal, line, 0.0), axis=1, keepdims=True)

    def merge(b, size, top, total, summed):
        tops = [column(ref, base, b)[:size] for ref, base in parts]
        high = functools.reduce(jnp.maximum, tops, top)
        weight = jnp.exp2(top - high)
        summed, total = weight * summed, weight * total
        for x, (ref, base) in zip(tops, parts):
            weight = jnp.exp2(x - high)
            summed = summed + weight * ref[base + b * HD:base + b * HD + size, :].astype(F32)
            total = total + weight
        return summed / total, high + jnp.log2(total)

    mine = jnp.concatenate([pos[...], pos[...]], 0)[:, 0:1]
    mask = where <= mine
    for b in range(4):
        rows = slice(b * HD, (b + 1) * HD)
        got, high = merge(b, HD, *prompt_part(q[rows, :], mask, keys, vals))
        value[rows, :] = got
        level[rows, :] = high
    key = jnp.concatenate([own_kv[0:DROWS, :]] * HEADS, 0)
    own = jnp.concatenate([own_kv[DROWS:2 * DROWS, :]] * HEADS, 0)
    top = jnp.sum(q[PR:QR, :].astype(F32) * key, axis=1, keepdims=True) * EXP
    got, high = merge(4, QR - PR, top, jnp.ones((QR - PR, HD), F32), own)
    for j in range(HEADS):
        out_d[:, j * HD:(j + 1) * HD] = got[j * DROWS:(j + 1) * DROWS].astype(BF16)


def final_kernel(q, far, value, level, pos, out_p, keys, vals):
    where = lay_out(far, keys, vals)
    mine = jnp.concatenate([pos[...], pos[...]], 0)[:, 0:1]
    mask = where <= mine
    for b in range(4):
        rows = slice(b * HD, (b + 1) * HD)
        top, total, summed = prompt_part(q[rows, :], mask, keys, vals)
        before = level[rows, :]
        high = jnp.maximum(top, before)
        left, right = jnp.exp2(before - high), jnp.exp2(top - high)
        merged = ((left * value[rows, :] + right * summed) / (left + right * total)).astype(BF16)
        out_p[:, 2 * b * HD:(2 * b + 1) * HD] = merged[:ROWS]
        out_p[:, (2 * b + 1) * HD:(2 * b + 2) * HD] = merged[ROWS:]


def last_call(kernel, arrays, outs, name):
    whole = pl.BlockSpec(memory_space=pltpu.VMEM)
    return pl.pallas_call(
        kernel,
        in_specs=[whole] * len(arrays),
        out_specs=[whole] * len(outs),
        out_shape=[jax.ShapeDtypeStruct(shape, dtype) for shape, dtype in outs],
        scratch_shapes=[pltpu.VMEM((NEAR * ROWS, HD), BF16), pltpu.VMEM((NEAR * ROWS, 2 * HD), BF16)],
        compiler_params=vmem(8),
        name=name,
    )(*arrays)


def body(
    prompt_hidden, kv_weight, cache_k, cache_v, prompt_q, dec_q, dec_k, dec_v,
    cache_lengths, prompt_pos, dec_owner,
):
    host = lax.axis_index("ctx").reshape(1)
    tp = lax.axis_index("tp").reshape(1)
    send, keep = project(tp, prompt_hidden, kv_weight)
    got = move(send, XLOW)
    kv_own, kv_give, q_own, own_kv, line, pos = pack(
        tie(tp, send), cache_lengths, dec_owner, prompt_pos, cache_k, cache_v, prompt_q, dec_q, dec_k, dec_v
    )
    kv_adj = move(kv_give, XADJ)
    kv_core = move(kv_own, CORE)
    q1 = move(q_own, Y1)
    q3 = move(q_own, Y3)

    send, keep = halve(4, tp, keep, got)
    got = move(send, Z6)
    q2 = move(tie(q_own, send), Y2)
    groups = ((q_own, q1), (q2, q3))
    state0 = cache_first(tie(host, send), groups[0], [kv_own, kv_core])
    got = tie(got, *state0)
    send, keep = halve(2, tp, keep, got)
    got = move(send, Z2)
    state1 = cache_first(tie(host, send), groups[1], [kv_own, kv_core])
    got = tie(got, kv_adj, *state1)
    half = (2 * ROWS, HD)
    send, total = glue(add_kernel, (), (keep, got), ((half, BF16), (half, F32)), "add")
    got = move(send, Z1)
    kv_diag = move(tie(kv_adj, send), CORE)
    back0 = cache_second(tie(host, send), groups[0], [kv_adj, kv_diag], state0)
    got = tie(got, *back0)
    piece, = glue(join_kernel, (), (total, got, line), (((PIECE, HD), BF16),), "join")
    got = move(piece, XFAR)
    back1 = cache_second(tie(host, piece), groups[1], [kv_adj, kv_diag], state1)
    got = tie(got, *back1)
    letter = ((PAIR + MSG, HD), BF16)
    letters = glue(letters_kernel, (), (piece, got, back0[1], *back1), (letter,) * 3, "letters")
    parts = [move(x, pairs) for x, pairs in zip(letters, (Y1, Y2, Y3))]
    near, = glue(near_kernel, (), (piece, got, *parts), (((4 * PAIR, HD), BF16),), "near")
    far = move(near, CORE)
    out_d, value, level = last_call(
        middle_kernel, (q_own, back0[0], *parts, near, own_kv, pos),
        [((DROWS, HEADS * HD), BF16), ((PR, HD), F32), ((PR, HD), F32)], "middle",
    )
    far = tie(far, level)
    out_p, = last_call(
        final_kernel, (q_own, far, value, level, pos), [((ROWS, HEADS * HD), BF16)], "final"
    )
    return out_p, out_d


def solution(mesh):
    in_specs = (
        P("ctx", "tp"), P("tp", None), P("ctx", None), P("ctx", None), P("ctx", "tp"),
        P("ctx", "tp"), P("ctx", None), P("ctx", None), P("ctx"), P("ctx"), P("ctx"),
    )
    out_specs = (P("ctx", "tp"), P("ctx", "tp"))
    return jax.shard_map(body, mesh=mesh, in_specs=in_specs, out_specs=out_specs, check_vma=False)
```

```python
import functools
import math

import jax
import jax.numpy as jnp
from jax import lax
from jax.experimental import pallas as pl
from jax.experimental.pallas import tpu as pltpu
from jax.sharding import PartitionSpec as P

HD = 128
HEADS = 8
KVH = 8
ROWS = 64
DROWS = 8
PR = HEADS * ROWS
QR = PR + HEADS * DROWS
MSG = QR + 16
SLOTS = 1024
CHUNK = 256
EXP = HD ** -0.5 * math.log2(math.e)
MASKED = -1e30
FLOOR = -1e20
BASE = 32
F32 = jnp.float32
BF16 = jnp.bfloat16


def swap(f):
    out = []
    for i in range(256):
        y, xh, core, xl, z = i // 64, i // 32 % 2, i // 16 % 2, i // 8 % 2, i % 8
        y, xh, core, xl, z = f(y, xh, core, xl, z)
        out.append((i, (((y * 2 + xh) * 2 + core) * 2 + xl) * 8 + z))
    return out


CORE = swap(lambda y, xh, c, xl, z: (y, xh, 1 - c, xl, z))
XADJ = swap(lambda y, xh, c, xl, z: (y, 1 - xh, c, 1 - xl, z))
XFAR = swap(lambda y, xh, c, xl, z: (y, 1 - xh, c, xl, z))
XLOW = swap(lambda y, xh, c, xl, z: (y, xh, c, 1 - xl, z))
Y1, Y2, Y3 = (swap(lambda y, xh, c, xl, z, k=k: (y ^ k, xh, c, xl, z)) for k in (1, 2, 3))
Z1, Z2, Z6 = (swap(lambda y, xh, c, xl, z, k=k: (y, xh, c, xl, z ^ k)) for k in (1, 2, 6))


def tie(x, *others):
    return lax.optimization_barrier((x, *others))[0]


def move(x, pairs):
    return lax.ppermute(x, ("ctx", "tp"), pairs)


LIGHT = pl.CostEstimate(flops=1, bytes_accessed=1, transcendentals=0)


def vmem(mib):
    return pltpu.CompilerParams(vmem_limit_bytes=mib * 1024 * 1024)


PARTS = 4
KV = 2 * SLOTS + 16
PIECE = 2 * ROWS + 16
PAIR = 2 * PIECE


def project_kernel(tp, h, w, send, keep, acc):
    side = tp[0] // 8
    deep = h.shape[1] // PARTS
    for i in range(PARTS):
        part = slice(i * deep, (i + 1) * deep)
        product = jnp.dot(h[:, part], w[part, :], preferred_element_type=F32)
        acc[...] = product if i == 0 else acc[...] + product
    for i in range(4):
        for out, where in ((send, 1 - side), (keep, side)):
            at = (where * 4 + i) * HD
            for v in range(2):
                block = acc[:, pl.ds(pl.multiple_of(at + v * KVH * HD, HD), HD)]
                out[i, v * ROWS:(v + 1) * ROWS, :] = block.astype(out.dtype)


def far_call(kernel, scalars, arrays, outs, scratch, name):
    whole = pl.BlockSpec(memory_space=pltpu.VMEM)
    return pl.pallas_call(
        kernel,
        in_specs=[pl.BlockSpec(memory_space=pltpu.SMEM)] * len(scalars)
        + [pl.BlockSpec(memory_space=pl.ANY)] * len(arrays),
        out_specs=[whole] * len(outs),
        out_shape=[jax.ShapeDtypeStruct(shape, dtype) for shape, dtype in outs],
        scratch_shapes=scratch,
        compiler_params=vmem(12),
        cost_estimate=LIGHT,
        name=name,
    )(*scalars, *[pltpu.with_memory_space_constraint(x, pltpu.HBM) for x in arrays])


def project(tp, hidden, weight):
    half = (4, 2 * ROWS, HD)
    whole = pl.BlockSpec(memory_space=pltpu.VMEM)
    return pl.pallas_call(
        project_kernel,
        in_specs=[pl.BlockSpec(memory_space=pltpu.SMEM), whole, whole],
        out_specs=[whole, whole],
        out_shape=[jax.ShapeDtypeStruct(half, BF16), jax.ShapeDtypeStruct(half, F32)],
        scratch_shapes=[pltpu.VMEM((ROWS, weight.shape[1]), F32)],
        compiler_params=vmem(8),
        name="project",
    )(tp, hidden, weight)


def pack_kernel(
    tp, lengths, owner, pos, cache_k, cache_v, prompt_q, dec_q, dec_k, dec_v,
    kv_own, kv_give, q_own, own_kv, pos_line, pos_column,
    c, pq, dq, dkv, owner_s, pos_s, sem_c, sem_s,
):
    head = tp[0] // 2
    own = pl.ds(pl.multiple_of(head * HD, HD), HD)
    other = pl.ds(pl.multiple_of((head ^ 4) * HD, HD), HD)
    copy = pltpu.make_async_copy
    copies = [
        copy(source, target, sem_s.at[i])
        for i, (source, target) in enumerate((
            (owner, owner_s), (pos, pos_s), (prompt_q, pq), (dec_q, dq),
            (dec_k.at[:, own], dkv.at[0]), (dec_v.at[:, own], dkv.at[1]),
        ))
    ]
    copies_c = [
        copy(source.at[:, part], c.at[i], sem_c.at[i])
        for i, (source, part) in enumerate(
            ((cache_k, other), (cache_v, other), (cache_k, own), (cache_v, own))
        )
    ]
    for x in copies + copies_c:
        x.start()
    for x in copies:
        x.wait()
    for j in range(HEADS):
        q_own[j * ROWS:(j + 1) * ROWS, :] = pq[:, j * HD:(j + 1) * HD]
    d = dq[...].astype(F32)
    rows = jnp.concatenate([d[:, j * HD:(j + 1) * HD] for j in range(HEADS)], 0)
    q_own[PR:QR, :] = rows.astype(BF16)
    row = lax.broadcasted_iota(jnp.int32, (16, HD), 0)
    who = jnp.zeros((16, HD), jnp.int32)
    for r in range(DROWS):
        who = jnp.where(row == r, owner_s[r], who)
    q_own[QR:MSG, :] = who.astype(F32).astype(BF16)
    lane = lax.broadcasted_iota(jnp.int32, (16, HD), 1) % ROWS
    eight = lax.broadcasted_iota(jnp.int32, (DROWS, HD), 0)
    line = jnp.zeros((16, HD), jnp.int32)
    for b in range(ROWS // DROWS):
        column = jnp.zeros((DROWS, HD), jnp.int32)
        for r in range(DROWS):
            column = jnp.where(eight == r, pos_s[b * DROWS + r], column)
            line = jnp.where(lane == b * DROWS + r, pos_s[b * DROWS + r], line)
        pos_column[b * DROWS:(b + 1) * DROWS, :] = column.astype(F32)
    line = jnp.where(row == 0, line // BASE, jnp.where(row == 1, line % BASE, 0))
    pos_line[...] = line.astype(F32).astype(BF16)
    own_kv[0:DROWS, :] = dkv[0].astype(F32)
    own_kv[DROWS:2 * DROWS, :] = dkv[1].astype(F32)

    n = lengths[0]
    value = jnp.where(row < 8, n // BASE, n % BASE).astype(F32).astype(BF16)
    filled = lax.broadcasted_iota(jnp.int32, (SLOTS, HD), 0) < n
    for i, out in enumerate((kv_give, kv_own)):
        copies_c[2 * i].wait()
        copies_c[2 * i + 1].wait()
        keys = c[2 * i].astype(F32)
        out[0:SLOTS, :] = jnp.where(filled, keys, keys[0:1]).astype(BF16)
        out[SLOTS:2 * SLOTS, :] = jnp.where(filled, c[2 * i + 1].astype(F32), 0.0).astype(BF16)
        out[2 * SLOTS:KV, :] = value


def pack(tp, lengths, *arrays):
    outs = [((KV, HD), BF16), ((KV, HD), BF16), ((MSG, HD), BF16), ((2 * DROWS, HD), F32), ((16, HD), BF16), ((ROWS, HD), F32)]
    scratch = [
        pltpu.VMEM((4, SLOTS, HD), BF16),
        pltpu.VMEM((ROWS, HEADS * HD), BF16),
        pltpu.VMEM((DROWS, HEADS * HD), BF16),
        pltpu.VMEM((2, DROWS, HD), BF16),
        pltpu.SMEM((DROWS,), jnp.int32),
        pltpu.SMEM((ROWS,), jnp.int32),
        pltpu.SemaphoreType.DMA((4,)),
        pltpu.SemaphoreType.DMA((6,)),
    ]
    return far_call(pack_kernel, (tp, lengths), arrays, outs, scratch, "pack")


def glue(kernel, scalars, arrays, outs, name):
    whole = pl.BlockSpec(memory_space=pltpu.VMEM)
    return pl.pallas_call(
        kernel,
        in_specs=[pl.BlockSpec(memory_space=pltpu.SMEM)] * len(scalars) + [whole] * len(arrays),
        out_specs=[whole] * len(outs),
        out_shape=[jax.ShapeDtypeStruct(shape, dtype) for shape, dtype in outs],
        compiler_params=vmem(4),
        cost_estimate=LIGHT,
        name=name,
    )(*scalars, *arrays)


def halve_kernel(bit, tp, keep, got, send, left):
    half = send.shape[0]
    mine = tp[0] // bit % 2
    for i in range(half):
        j = (1 - mine) * half + i
        send[i] = (keep[j] + got[j].astype(F32)).astype(BF16)
        j = mine * half + i
        left[i] = keep[j] + got[j].astype(F32)


def halve(bit, tp, keep, got):
    shape = (keep.shape[0] // 2,) + keep.shape[1:]
    return glue(functools.partial(halve_kernel, bit), (tp,), (keep, got), ((shape, BF16), (shape, F32)), "halve")


def add_kernel(keep, got, send, total):
    x = keep[0] + got[0].astype(F32)
    send[...] = x.astype(BF16)
    total[...] = x


def join_kernel(total, got, line, piece):
    piece[0:2 * ROWS, :] = (total[...] + got[...].astype(F32)).astype(BF16)
    piece[2 * ROWS:PIECE, :] = line[...]


def letters_kernel(piece, got, back, pair, letter):
    for out in (pair, letter):
        out[0:PIECE, :] = piece[...]
        out[PIECE:PAIR, :] = got[...]
    letter[PAIR:PAIR + MSG, :] = back[...]


def near_kernel(pair, g1, g2, m3, out):
    for i, m in enumerate((pair, g1, g2, m3)):
        out[i * PAIR:(i + 1) * PAIR, :] = m[0:PAIR, :]


BLOCK = 192


def absorb(ctx, n, kv, qs, acc, top):
    tail = kv[2 * SLOTS:2 * SLOTS + 16, :].astype(F32)
    length = jnp.max(tail[:8] * BASE + tail[8:]).astype(jnp.int32)
    host = (ctx[0] ^ n).astype(F32)

    def chunk(base, size):
        k = kv[pl.ds(pl.multiple_of(base, 256), size), :]
        v = kv[pl.ds(pl.multiple_of(SLOTS + base, 256), size), :]
        one = lax.broadcasted_iota(jnp.int32, (size, HD), 0) < length - base
        v = jnp.concatenate([v, jnp.where(one, 1.0, 0.0).astype(BF16)], 1)
        for g, q in enumerate(qs):
            for start in range(0, QR, BLOCK):
                rows = slice(g * QR + start, g * QR + start + BLOCK)
                s = lax.dot_general(
                    q[start:start + BLOCK, :], k, (((1,), (1,)), ((), ())), preferred_element_type=F32
                )
                old = top[rows, :]
                new = jnp.maximum(old, jnp.max(s, axis=1, keepdims=True))
                less = new
                if start + BLOCK > PR:
                    owner = q[QR:MSG, :].astype(F32)[:DROWS]
                    owner = jnp.concatenate([jnp.full((BLOCK - QR + PR, HD), 99.0)] + [owner] * HEADS, 0)
                    seen = owner >= host
                    new = jnp.where(seen, new, old)
                    less = jnp.where(seen, new, -MASKED)
                p = jnp.exp2((s - jnp.concatenate([less] * (size // HD), 1)) * EXP)
                shrink = jnp.exp2((old - new) * EXP)
                acc[rows, :] = acc[rows, :] * jnp.concatenate([shrink, shrink], 1) + jnp.dot(
                    p.astype(BF16), v, preferred_element_type=F32
                )
                top[rows, :] = new

    rest = length % 512
    full = length // 512 + (rest > 256).astype(jnp.int32)

    def step(c, carry):
        chunk(c * 512, 512)
        return carry

    lax.fori_loop(0, full, step, 0)

    @pl.when((rest > 0) & (rest <= 256))
    def _():
        chunk(full * 512, 256)


def first_kernel(ctx, q0, q1, kv0, kv1, acc, top):
    acc[...] = jnp.zeros_like(acc)
    top[...] = jnp.full_like(top, FLOOR)
    for n, kv in enumerate((kv0, kv1)):
        absorb(ctx, n, kv, (q0, q1), acc, top)


def second_kernel(ctx, q0, q1, kv2, kv3, acc0, top0, out0, out1, acc, top):
    acc[...] = acc0[...]
    top[...] = top0[...]
    for n, kv in enumerate((kv2, kv3)):
        absorb(ctx, n + 2, kv, (q0, q1), acc, top)
    diagonal = lax.broadcasted_iota(jnp.int32, (HD, HD), 0) == lax.broadcasted_iota(jnp.int32, (HD, HD), 1)
    index = lax.broadcasted_iota(jnp.int32, (16, HD), 0)
    for g, out in enumerate((out0, out1)):
        rows = slice(g * QR, (g + 1) * QR)
        total = acc[rows, HD:]
        some = total > 0.0
        total = jnp.where(some, total, 1.0)
        out[0:QR, :] = jnp.where(some, acc[rows, :HD] / total, 0.0).astype(BF16)
        level = jnp.where(some, top[rows, :] * EXP + jnp.log2(total), FLOOR)
        packed = jnp.zeros((16, HD), F32)
        for b in range(5):
            block = level[b * HD:(b + 1) * HD, :]
            if b == 4:
                block = jnp.concatenate([block, jnp.zeros((HD - QR + PR, HD), F32)], 0)
            line = jnp.sum(jnp.where(diagonal, block, 0.0), axis=0, keepdims=True)
            for i in range(3):
                piece = line.astype(BF16).astype(F32)
                packed = jnp.where(index == 3 * b + i, piece, packed)
                line = line - piece
        out[QR:MSG, :] = packed.astype(BF16)


STATE = ((2 * QR, 2 * HD), (2 * QR, HD))


def cache_call(kernel, host, arrays, outs, scratch, name):
    whole = pl.BlockSpec(memory_space=pltpu.VMEM)
    return pl.pallas_call(
        kernel,
        in_specs=[pl.BlockSpec(memory_space=pltpu.SMEM)] + [whole] * len(arrays),
        out_specs=[whole] * len(outs),
        out_shape=[jax.ShapeDtypeStruct(shape, dtype) for shape, dtype in outs],
        scratch_shapes=[pltpu.VMEM(shape, F32) for shape in scratch],
        compiler_params=vmem(8),
        cost_estimate=LIGHT,
        name=name,
    )(host, *arrays)


def cache_first(host, qs, kvs):
    return cache_call(first_kernel, host, (*qs, *kvs), [(x, F32) for x in STATE], (), "cache_first")


def cache_second(host, qs, kvs, state):
    return cache_call(
        second_kernel, host, (*qs, *kvs, *state), [((MSG, HD), BF16)] * 2, STATE, "cache_second"
    )


NEAR = 8


def lay_out(ref, keys, vals):
    vals[:, HD:] = jnp.ones((NEAR * ROWS, HD), BF16)
    lane = lax.broadcasted_iota(jnp.int32, (1, HD), 1)
    lines = []
    for i in range(NEAR):
        at = i * ROWS
        base = i * PIECE
        keys[at:at + ROWS, :] = ref[base:base + ROWS, :]
        vals[at:at + ROWS, 0:HD] = ref[base + ROWS:base + 2 * ROWS, :]
        tail = ref[base + 2 * ROWS:base + PIECE, :].astype(F32)
        lines.append(tail[0:1] * BASE + tail[1:2])
    return jnp.concatenate(
        [jnp.where(lane < ROWS, lines[2 * i], lines[2 * i + 1]) for i in range(NEAR // 2)], 1
    )


def prompt_part(q, mask, keys, vals):
    s = lax.dot_general(q, keys[...], (((1,), (1,)), ((), ())), preferred_element_type=F32)
    s = jnp.where(mask, s, MASKED)
    high = jnp.maximum(jnp.max(s, axis=1, keepdims=True), FLOOR)
    p = jnp.exp2((s - high) * EXP)
    o = jnp.dot(p.astype(BF16), vals[...], preferred_element_type=F32)
    return high * EXP, o[:, HD:], o[:, :HD]


def middle_kernel(q, m0, m1, m2, m3, near, own_kv, pos, out_d, value, level, keys, vals):
    parts = ((m0, 0), (m1, 0), (m2, 0), (m3, PAIR))
    where = lay_out(near, keys, vals)
    diagonal = lax.broadcasted_iota(jnp.int32, (HD, HD), 0) == lax.broadcasted_iota(jnp.int32, (HD, HD), 1)

    def column(ref, base, b):
        tail = ref[base + QR:base + MSG, :].astype(F32)
        line = tail[3 * b:3 * b + 1] + tail[3 * b + 1:3 * b + 2] + tail[3 * b + 2:3 * b + 3]
        return jnp.sum(jnp.where(diagonal, line, 0.0), axis=1, keepdims=True)

    def merge(b, size, top, total, summed):
        tops = [column(ref, base, b)[:size] for ref, base in parts]
        high = functools.reduce(jnp.maximum, tops, top)
        weight = jnp.exp2(top - high)
        summed, total = weight * summed, weight * total
        for x, (ref, base) in zip(tops, parts):
            weight = jnp.exp2(x - high)
            summed = summed + weight * ref[base + b * HD:base + b * HD + size, :].astype(F32)
            total = total + weight
        return summed / total, high + jnp.log2(total)

    mine = jnp.concatenate([pos[...], pos[...]], 0)[:, 0:1]
    mask = where <= mine
    for b in range(4):
        rows = slice(b * HD, (b + 1) * HD)
        got, high = merge(b, HD, *prompt_part(q[rows, :], mask, keys, vals))
        value[rows, :] = got
        level[rows, :] = high
    key = jnp.concatenate([own_kv[0:DROWS, :]] * HEADS, 0)
    own = jnp.concatenate([own_kv[DROWS:2 * DROWS, :]] * HEADS, 0)
    top = jnp.sum(q[PR:QR, :].astype(F32) * key, axis=1, keepdims=True) * EXP
    got, high = merge(4, QR - PR, top, jnp.ones((QR - PR, HD), F32), own)
    for j in range(HEADS):
        out_d[:, j * HD:(j + 1) * HD] = got[j * DROWS:(j + 1) * DROWS].astype(BF16)


def final_kernel(q, far, value, level, pos, out_p, keys, vals):
    where = lay_out(far, keys, vals)
    mine = jnp.concatenate([pos[...], pos[...]], 0)[:, 0:1]
    mask = where <= mine
    for b in range(4):
        rows = slice(b * HD, (b + 1) * HD)
        top, total, summed = prompt_part(q[rows, :], mask, keys, vals)
        before = level[rows, :]
        high = jnp.maximum(top, before)
        left, right = jnp.exp2(before - high), jnp.exp2(top - high)
        merged = ((left * value[rows, :] + right * summed) / (left + right * total)).astype(BF16)
        out_p[:, 2 * b * HD:(2 * b + 1) * HD] = merged[:ROWS]
        out_p[:, (2 * b + 1) * HD:(2 * b + 2) * HD] = merged[ROWS:]


def last_call(kernel, arrays, outs, name):
    whole = pl.BlockSpec(memory_space=pltpu.VMEM)
    return pl.pallas_call(
        kernel,
        in_specs=[whole] * len(arrays),
        out_specs=[whole] * len(outs),
        out_shape=[jax.ShapeDtypeStruct(shape, dtype) for shape, dtype in outs],
        scratch_shapes=[pltpu.VMEM((NEAR * ROWS, HD), BF16), pltpu.VMEM((NEAR * ROWS, 2 * HD), BF16)],
        compiler_params=vmem(8),
        cost_estimate=LIGHT,
        name=name,
    )(*arrays)


def body(
    prompt_hidden, kv_weight, cache_k, cache_v, prompt_q, dec_q, dec_k, dec_v,
    cache_lengths, prompt_pos, dec_owner,
):
    host = lax.axis_index("ctx").reshape(1)
    tp = lax.axis_index("tp").reshape(1)
    send, keep = project(tp, prompt_hidden, kv_weight)
    got = move(send, XLOW)
    kv_own, kv_give, q_own, own_kv, line, pos = pack(
        tp, cache_lengths, dec_owner, prompt_pos, cache_k, cache_v, prompt_q, dec_q, dec_k, dec_v
    )
    kv_adj = move(kv_give, XADJ)
    kv_core = move(kv_own, CORE)
    q1 = move(q_own, Y1)
    q3 = move(q_own, Y3)

    send, keep = halve(4, tp, keep, got)
    got = move(send, Z6)
    q2 = move(q_own, Y2)
    groups = ((q1, q2), (q_own, q3))
    state0 = cache_first(tie(host, send), groups[0], [kv_own, kv_core])
    got = tie(got, *state0)
    send, keep = halve(2, tp, keep, got)
    got = move(send, Z2)
    kv_diag = move(tie(kv_adj, send), CORE)
    back0 = cache_second(tie(host, send), groups[0], [kv_adj, kv_diag], state0)
    got = tie(got, *back0)
    half = (2 * ROWS, HD)
    send, total = glue(add_kernel, (), (keep, got), ((half, BF16), (half, F32)), "add")
    got = move(send, Z1)
    m2 = move(tie(back0[1], send), Y2)
    state1 = cache_first(tie(host, send), groups[1], [kv_own, kv_core])
    got = tie(got, *state1)
    piece, = glue(join_kernel, (), (total, got, line), (((PIECE, HD), BF16),), "join")
    got = move(piece, XFAR)
    m1 = move(tie(back0[0], piece), Y1)
    back1 = cache_second(tie(host, piece), groups[1], [kv_adj, kv_diag], state1)
    got = tie(got, m1, m2, *back1)
    mine, back3 = back1
    pair, letter = glue(
        letters_kernel, (), (piece, got, back3), (((PAIR, HD), BF16), ((PAIR + MSG, HD), BF16)), "letters"
    )
    g2, g1, m3 = move(pair, Y2), move(pair, Y1), move(letter, Y3)
    near, = glue(near_kernel, (), (pair, g1, g2, m3), (((4 * PAIR, HD), BF16),), "near")
    far = move(near, CORE)
    out_d, value, level = last_call(
        middle_kernel, (q_own, mine, m1, m2, m3, near, own_kv, pos),
        [((DROWS, HEADS * HD), BF16), ((PR, HD), F32), ((PR, HD), F32)], "middle",
    )
    far = tie(far, level)
    out_p, = last_call(
        final_kernel, (q_own, far, value, level, pos), [((ROWS, HEADS * HD), BF16)], "final"
    )
    return out_p, out_d


def solution(mesh):
    in_specs = (
        P("ctx", "tp"), P("tp", None), P("ctx", None), P("ctx", None), P("ctx", "tp"),
        P("ctx", "tp"), P("ctx", None), P("ctx", None), P("ctx"), P("ctx"), P("ctx"),
    )
    out_specs = (P("ctx", "tp"), P("ctx", "tp"))
    return jax.shard_map(body, mesh=mesh, in_specs=in_specs, out_specs=out_specs, check_vma=False)
```

```python
import functools
import math

import jax
import jax.numpy as jnp
from jax import lax
from jax.experimental import pallas as pl
from jax.experimental.pallas import tpu as pltpu
from jax.sharding import PartitionSpec as P

HD = 128
HEADS = 8
KVH = 8
ROWS = 64
DROWS = 8
PR = HEADS * ROWS
QR = PR + HEADS * DROWS
MSG = QR + 16
SLOTS = 1024
CHUNK = 256
EXP = HD ** -0.5 * math.log2(math.e)
MASKED = -1e30
FLOOR = -1e20
BASE = 32
F32 = jnp.float32
BF16 = jnp.bfloat16


def swap(f):
    out = []
    for i in range(256):
        y, xh, core, xl, z = i // 64, i // 32 % 2, i // 16 % 2, i // 8 % 2, i % 8
        y, xh, core, xl, z = f(y, xh, core, xl, z)
        out.append((i, (((y * 2 + xh) * 2 + core) * 2 + xl) * 8 + z))
    return out


CORE = swap(lambda y, xh, c, xl, z: (y, xh, 1 - c, xl, z))
XADJ = swap(lambda y, xh, c, xl, z: (y, 1 - xh, c, 1 - xl, z))
XFAR = swap(lambda y, xh, c, xl, z: (y, 1 - xh, c, xl, z))
XLOW = swap(lambda y, xh, c, xl, z: (y, xh, c, 1 - xl, z))
Y1, Y2, Y3 = (swap(lambda y, xh, c, xl, z, k=k: (y ^ k, xh, c, xl, z)) for k in (1, 2, 3))
Z1, Z2, Z6 = (swap(lambda y, xh, c, xl, z, k=k: (y, xh, c, xl, z ^ k)) for k in (1, 2, 6))


def tie(x, *others):
    return lax.optimization_barrier((x, *others))[0]


def move(x, pairs):
    return lax.ppermute(x, ("ctx", "tp"), pairs)


LIGHT = pl.CostEstimate(flops=1, bytes_accessed=1, transcendentals=0)


def vmem(mib):
    return pltpu.CompilerParams(vmem_limit_bytes=mib * 1024 * 1024)


PARTS = 4
KV = 2 * SLOTS + 16
PIECE = 2 * ROWS + 16
PAIR = 2 * PIECE


def project_kernel(tp, h, w, send, keep, acc):
    side = tp[0] // 8
    deep = h.shape[1] // PARTS
    for i in range(PARTS):
        part = slice(i * deep, (i + 1) * deep)
        product = jnp.dot(h[:, part], w[part, :], preferred_element_type=F32)
        acc[...] = product if i == 0 else acc[...] + product
    for i in range(4):
        for out, where in ((send, 1 - side), (keep, side)):
            at = (where * 4 + i) * HD
            for v in range(2):
                block = acc[:, pl.ds(pl.multiple_of(at + v * KVH * HD, HD), HD)]
                out[i, v * ROWS:(v + 1) * ROWS, :] = block.astype(out.dtype)


def far_call(kernel, scalars, arrays, outs, scratch, name):
    whole = pl.BlockSpec(memory_space=pltpu.VMEM)
    return pl.pallas_call(
        kernel,
        in_specs=[pl.BlockSpec(memory_space=pltpu.SMEM)] * len(scalars)
        + [pl.BlockSpec(memory_space=pl.ANY)] * len(arrays),
        out_specs=[whole] * len(outs),
        out_shape=[jax.ShapeDtypeStruct(shape, dtype) for shape, dtype in outs],
        scratch_shapes=scratch,
        compiler_params=vmem(12),
        cost_estimate=LIGHT,
        name=name,
    )(*scalars, *[pltpu.with_memory_space_constraint(x, pltpu.HBM) for x in arrays])


def project(tp, hidden, weight):
    half = (4, 2 * ROWS, HD)
    whole = pl.BlockSpec(memory_space=pltpu.VMEM)
    return pl.pallas_call(
        project_kernel,
        in_specs=[pl.BlockSpec(memory_space=pltpu.SMEM), whole, whole],
        out_specs=[whole, whole],
        out_shape=[jax.ShapeDtypeStruct(half, BF16), jax.ShapeDtypeStruct(half, F32)],
        scratch_shapes=[pltpu.VMEM((ROWS, weight.shape[1]), F32)],
        compiler_params=vmem(8),
        name="project",
    )(tp, hidden, weight)


def pack_kernel(
    tp, lengths, owner, pos, cache_k, cache_v, prompt_q, dec_q, dec_k, dec_v,
    kv_own, kv_give, q_own, own_kv, pos_line, pos_column,
    c, pq, dq, dkv, owner_s, pos_s, sem_c, sem_s,
):
    head = tp[0] // 2
    own = pl.ds(pl.multiple_of(head * HD, HD), HD)
    other = pl.ds(pl.multiple_of((head ^ 4) * HD, HD), HD)
    copy = pltpu.make_async_copy
    copies = [
        copy(source, target, sem_s.at[i])
        for i, (source, target) in enumerate((
            (owner, owner_s), (pos, pos_s), (prompt_q, pq), (dec_q, dq),
            (dec_k.at[:, own], dkv.at[0]), (dec_v.at[:, own], dkv.at[1]),
        ))
    ]
    copies_c = [
        copy(source.at[:, part], c.at[i], sem_c.at[i])
        for i, (source, part) in enumerate(
            ((cache_k, other), (cache_v, other), (cache_k, own), (cache_v, own))
        )
    ]
    for x in copies + copies_c:
        x.start()
    for x in copies:
        x.wait()
    for j in range(HEADS):
        q_own[j * ROWS:(j + 1) * ROWS, :] = pq[:, j * HD:(j + 1) * HD]
    d = dq[...].astype(F32)
    rows = jnp.concatenate([d[:, j * HD:(j + 1) * HD] for j in range(HEADS)], 0)
    q_own[PR:QR, :] = rows.astype(BF16)
    row = lax.broadcasted_iota(jnp.int32, (16, HD), 0)
    who = jnp.zeros((16, HD), jnp.int32)
    for r in range(DROWS):
        who = jnp.where(row == r, owner_s[r], who)
    q_own[QR:MSG, :] = who.astype(F32).astype(BF16)
    lane = lax.broadcasted_iota(jnp.int32, (16, HD), 1) % ROWS
    eight = lax.broadcasted_iota(jnp.int32, (DROWS, HD), 0)
    line = jnp.zeros((16, HD), jnp.int32)
    for b in range(ROWS // DROWS):
        column = jnp.zeros((DROWS, HD), jnp.int32)
        for r in range(DROWS):
            column = jnp.where(eight == r, pos_s[b * DROWS + r], column)
            line = jnp.where(lane == b * DROWS + r, pos_s[b * DROWS + r], line)
        pos_column[b * DROWS:(b + 1) * DROWS, :] = column.astype(F32)
    line = jnp.where(row == 0, line // BASE, jnp.where(row == 1, line % BASE, 0))
    pos_line[...] = line.astype(F32).astype(BF16)
    own_kv[0:DROWS, :] = dkv[0].astype(F32)
    own_kv[DROWS:2 * DROWS, :] = dkv[1].astype(F32)

    n = lengths[0]
    value = jnp.where(row < 8, n // BASE, n % BASE).astype(F32).astype(BF16)
    filled = lax.broadcasted_iota(jnp.int32, (SLOTS, HD), 0) < n
    for i, out in enumerate((kv_give, kv_own)):
        copies_c[2 * i].wait()
        copies_c[2 * i + 1].wait()
        keys = c[2 * i].astype(F32)
        out[0:SLOTS, :] = jnp.where(filled, keys, keys[0:1]).astype(BF16)
        out[SLOTS:2 * SLOTS, :] = jnp.where(filled, c[2 * i + 1].astype(F32), 0.0).astype(BF16)
        out[2 * SLOTS:KV, :] = value


def pack(tp, lengths, *arrays):
    outs = [((KV, HD), BF16), ((KV, HD), BF16), ((MSG, HD), BF16), ((2 * DROWS, HD), F32), ((16, HD), BF16), ((ROWS, HD), F32)]
    scratch = [
        pltpu.VMEM((4, SLOTS, HD), BF16),
        pltpu.VMEM((ROWS, HEADS * HD), BF16),
        pltpu.VMEM((DROWS, HEADS * HD), BF16),
        pltpu.VMEM((2, DROWS, HD), BF16),
        pltpu.SMEM((DROWS,), jnp.int32),
        pltpu.SMEM((ROWS,), jnp.int32),
        pltpu.SemaphoreType.DMA((4,)),
        pltpu.SemaphoreType.DMA((6,)),
    ]
    return far_call(pack_kernel, (tp, lengths), arrays, outs, scratch, "pack")


def glue(kernel, scalars, arrays, outs, name):
    whole = pl.BlockSpec(memory_space=pltpu.VMEM)
    return pl.pallas_call(
        kernel,
        in_specs=[pl.BlockSpec(memory_space=pltpu.SMEM)] * len(scalars) + [whole] * len(arrays),
        out_specs=[whole] * len(outs),
        out_shape=[jax.ShapeDtypeStruct(shape, dtype) for shape, dtype in outs],
        compiler_params=vmem(4),
        cost_estimate=LIGHT,
        name=name,
    )(*scalars, *arrays)


def halve_kernel(bit, tp, keep, got, send, left):
    half = send.shape[0]
    mine = tp[0] // bit % 2
    for i in range(half):
        j = (1 - mine) * half + i
        send[i] = (keep[j] + got[j].astype(F32)).astype(BF16)
        j = mine * half + i
        left[i] = keep[j] + got[j].astype(F32)


def halve(bit, tp, keep, got):
    shape = (keep.shape[0] // 2,) + keep.shape[1:]
    return glue(functools.partial(halve_kernel, bit), (tp,), (keep, got), ((shape, BF16), (shape, F32)), "halve")


def add_kernel(keep, got, send, total):
    x = keep[0] + got[0].astype(F32)
    send[...] = x.astype(BF16)
    total[...] = x


def join_kernel(total, got, line, piece):
    piece[0:2 * ROWS, :] = (total[...] + got[...].astype(F32)).astype(BF16)
    piece[2 * ROWS:PIECE, :] = line[...]


def pair_kernel(piece, got, out):
    out[0:PIECE, :] = piece[...]
    out[PIECE:PAIR, :] = got[...]


def near_kernel(pair, g1, g2, g3, out):
    for i, m in enumerate((pair, g1, g2, g3)):
        out[i * PAIR:(i + 1) * PAIR, :] = m[...]


BLOCK = 192
BATCH = 9


def absorb(ctx, n, kv, qs, acc, top):
    tail = kv[2 * SLOTS:2 * SLOTS + 16, :].astype(F32)
    length = jnp.max(tail[:8] * BASE + tail[8:]).astype(jnp.int32)
    host = (ctx[0] ^ n).astype(F32)

    def chunk(base, size):
        k = kv[pl.ds(pl.multiple_of(base, 256), size), :]
        v = kv[pl.ds(pl.multiple_of(SLOTS + base, 256), size), :]
        one = lax.broadcasted_iota(jnp.int32, (size, HD), 0) < length - base
        v = jnp.concatenate([v, jnp.where(one, 1.0, 0.0).astype(BF16)], 1)
        blocks = [(g, q, start) for g, q in enumerate(qs) for start in range(0, QR, BLOCK)]
        for first in range(0, len(blocks), BATCH):
            batch = blocks[first:first + BATCH]
            scores = [
                lax.dot_general(
                    q[start:start + BLOCK, :], k, (((1,), (1,)), ((), ())), preferred_element_type=F32
                )
                for g, q, start in batch
            ]
            weights = []
            for (g, q, start), s in zip(batch, scores):
                rows = slice(g * QR + start, g * QR + start + BLOCK)
                old = top[rows, :]
                new = jnp.maximum(old, jnp.max(s, axis=1, keepdims=True))
                less = new
                if start + BLOCK > PR:
                    owner = q[QR:MSG, :].astype(F32)[:DROWS]
                    owner = jnp.concatenate([jnp.full((BLOCK - QR + PR, HD), 99.0)] + [owner] * HEADS, 0)
                    seen = owner >= host
                    new = jnp.where(seen, new, old)
                    less = jnp.where(seen, new, -MASKED)
                p = jnp.exp2((s - jnp.concatenate([less] * (size // HD), 1)) * EXP)
                shrink = jnp.exp2((old - new) * EXP)
                top[rows, :] = new
                weights.append((rows, p.astype(BF16), shrink))
            for rows, p, shrink in weights:
                acc[rows, :] = acc[rows, :] * jnp.concatenate([shrink, shrink], 1) + jnp.dot(
                    p, v, preferred_element_type=F32
                )

    rest = length % 512
    full = length // 512 + (rest > 256).astype(jnp.int32)

    def step(c, carry):
        chunk(c * 512, 512)
        return carry

    lax.fori_loop(0, full, step, 0)

    @pl.when((rest > 0) & (rest <= 256))
    def _():
        chunk(full * 512, 256)


def attend_kernel(ctx, *refs, groups, hosts, begin, end):
    qs, kvs, refs = refs[:groups], refs[groups:groups + len(hosts)], refs[groups + len(hosts):]
    before, refs = ((), refs) if begin else (refs[:2], refs[2:])
    outs, (acc, top) = refs[:-2], refs[-2:]
    acc[...] = jnp.zeros_like(acc) if begin else before[0][...]
    top[...] = jnp.full_like(top, FLOOR) if begin else before[1][...]
    for n, kv in zip(hosts, kvs):
        absorb(ctx, n, kv, qs, acc, top)
    if not end:
        return
    diagonal = lax.broadcasted_iota(jnp.int32, (HD, HD), 0) == lax.broadcasted_iota(jnp.int32, (HD, HD), 1)
    index = lax.broadcasted_iota(jnp.int32, (16, HD), 0)
    for g, out in enumerate(outs):
        rows = slice(g * QR, (g + 1) * QR)
        total = acc[rows, HD:]
        out[0:QR, :] = (acc[rows, :HD] / jnp.where(total > 0.0, total, 1.0)).astype(BF16)
        packed = jnp.zeros((16, HD), F32)
        for b in range(5):
            low = g * QR + b * HD
            lines = []
            for ref, column in ((acc, HD), (top, 0)):
                block = ref[low:low + min(HD, QR - b * HD), column:column + HD]
                if b == 4:
                    block = jnp.concatenate([block, jnp.zeros((HD - QR + PR, HD), F32)], 0)
                lines.append(jnp.sum(jnp.where(diagonal, block, 0.0), axis=0, keepdims=True))
            some = lines[0] > 0.0
            line = jnp.where(some, lines[1] * EXP + jnp.log2(jnp.where(some, lines[0], 1.0)), FLOOR)
            for i in range(3):
                piece = line.astype(BF16).astype(F32)
                packed = jnp.where(index == 3 * b + i, piece, packed)
                line = line - piece
        out[QR:MSG, :] = packed.astype(BF16)


def attend(host, qs, hosts, kvs, state=(), end=False):
    whole = pl.BlockSpec(memory_space=pltpu.VMEM)
    shapes = ((len(qs) * QR, 2 * HD), (len(qs) * QR, HD))
    outs = [((MSG, HD), BF16)] * len(qs) if end else [(x, F32) for x in shapes]
    arrays = (*qs, *kvs, *state)
    return pl.pallas_call(
        functools.partial(attend_kernel, groups=len(qs), hosts=hosts, begin=not state, end=end),
        in_specs=[pl.BlockSpec(memory_space=pltpu.SMEM)] + [whole] * len(arrays),
        out_specs=[whole] * len(outs),
        out_shape=[jax.ShapeDtypeStruct(shape, dtype) for shape, dtype in outs],
        scratch_shapes=[pltpu.VMEM(shape, F32) for shape in shapes] if end else [],
        compiler_params=vmem(16),
        cost_estimate=LIGHT,
        name="attend",
    )(host, *arrays)


NEAR = 8


def lay_out(ref, keys, vals):
    vals[:, HD:] = jnp.ones((NEAR * ROWS, HD), BF16)
    lane = lax.broadcasted_iota(jnp.int32, (1, HD), 1)
    lines = []
    for i in range(NEAR):
        at = i * ROWS
        base = i * PIECE
        keys[at:at + ROWS, :] = ref[base:base + ROWS, :]
        vals[at:at + ROWS, 0:HD] = ref[base + ROWS:base + 2 * ROWS, :]
        tail = ref[base + 2 * ROWS:base + PIECE, :].astype(F32)
        lines.append(tail[0:1] * BASE + tail[1:2])
    return jnp.concatenate(
        [jnp.where(lane < ROWS, lines[2 * i], lines[2 * i + 1]) for i in range(NEAR // 2)], 1
    )


def prompt_part(q, mask, keys, vals):
    s = lax.dot_general(q, keys[...], (((1,), (1,)), ((), ())), preferred_element_type=F32)
    s = jnp.where(mask, s, MASKED)
    high = jnp.maximum(jnp.max(s, axis=1, keepdims=True), FLOOR)
    p = jnp.exp2((s - high) * EXP)
    o = jnp.dot(p.astype(BF16), vals[...], preferred_element_type=F32)
    return high * EXP, o[:, HD:], o[:, :HD]


def middle_kernel(q, m0, m1, m2, m3, near, own_kv, pos, out_d, value, level, keys, vals):
    parts = ((m0, 0), (m1, 0), (m2, 0), (m3, 0))
    where = lay_out(near, keys, vals)
    diagonal = lax.broadcasted_iota(jnp.int32, (HD, HD), 0) == lax.broadcasted_iota(jnp.int32, (HD, HD), 1)

    def column(ref, base, b):
        tail = ref[base + QR:base + MSG, :].astype(F32)
        line = tail[3 * b:3 * b + 1] + tail[3 * b + 1:3 * b + 2] + tail[3 * b + 2:3 * b + 3]
        return jnp.sum(jnp.where(diagonal, line, 0.0), axis=1, keepdims=True)

    def merge(b, size, top, total, summed):
        tops = [column(ref, base, b)[:size] for ref, base in parts]
        high = functools.reduce(jnp.maximum, tops, top)
        weight = jnp.exp2(top - high)
        summed, total = weight * summed, weight * total
        for x, (ref, base) in zip(tops, parts):
            weight = jnp.exp2(x - high)
            summed = summed + weight * ref[base + b * HD:base + b * HD + size, :].astype(F32)
            total = total + weight
        return summed / total, high + jnp.log2(total)

    mine = jnp.concatenate([pos[...], pos[...]], 0)[:, 0:1]
    mask = where <= mine
    for b in range(4):
        rows = slice(b * HD, (b + 1) * HD)
        got, high = merge(b, HD, *prompt_part(q[rows, :], mask, keys, vals))
        value[rows, :] = got
        level[rows, :] = high
    key = jnp.concatenate([own_kv[0:DROWS, :]] * HEADS, 0)
    own = jnp.concatenate([own_kv[DROWS:2 * DROWS, :]] * HEADS, 0)
    top = jnp.sum(q[PR:QR, :].astype(F32) * key, axis=1, keepdims=True) * EXP
    got, high = merge(4, QR - PR, top, jnp.ones((QR - PR, HD), F32), own)
    for j in range(HEADS):
        out_d[:, j * HD:(j + 1) * HD] = got[j * DROWS:(j + 1) * DROWS].astype(BF16)


def final_kernel(q, far, value, level, pos, out_p, keys, vals):
    where = lay_out(far, keys, vals)
    mine = jnp.concatenate([pos[...], pos[...]], 0)[:, 0:1]
    mask = where <= mine
    for b in range(4):
        rows = slice(b * HD, (b + 1) * HD)
        top, total, summed = prompt_part(q[rows, :], mask, keys, vals)
        before = level[rows, :]
        high = jnp.maximum(top, before)
        left, right = jnp.exp2(before - high), jnp.exp2(top - high)
        merged = ((left * value[rows, :] + right * summed) / (left + right * total)).astype(BF16)
        out_p[:, 2 * b * HD:(2 * b + 1) * HD] = merged[:ROWS]
        out_p[:, (2 * b + 1) * HD:(2 * b + 2) * HD] = merged[ROWS:]


def last_call(kernel, arrays, outs, name):
    whole = pl.BlockSpec(memory_space=pltpu.VMEM)
    return pl.pallas_call(
        kernel,
        in_specs=[whole] * len(arrays),
        out_specs=[whole] * len(outs),
        out_shape=[jax.ShapeDtypeStruct(shape, dtype) for shape, dtype in outs],
        scratch_shapes=[pltpu.VMEM((NEAR * ROWS, HD), BF16), pltpu.VMEM((NEAR * ROWS, 2 * HD), BF16)],
        compiler_params=vmem(8),
        cost_estimate=LIGHT,
        name=name,
    )(*arrays)


def body(
    prompt_hidden, kv_weight, cache_k, cache_v, prompt_q, dec_q, dec_k, dec_v,
    cache_lengths, prompt_pos, dec_owner,
):
    host = lax.axis_index("ctx").reshape(1)
    tp = lax.axis_index("tp").reshape(1)
    send, keep = project(tp, prompt_hidden, kv_weight)
    kv_own, kv_give, q_own, own_kv, line, pos = pack(
        tp, cache_lengths, dec_owner, prompt_pos, cache_k, cache_v, prompt_q, dec_q, dec_k, dec_v
    )
    kv_adj = move(kv_give, XADJ)
    kv_core = move(kv_own, CORE)
    got = move(tie(send, kv_core), XLOW)
    q1 = move(q_own, Y1)
    q2, q3 = move(q_own, Y2), move(q_own, Y3)

    send, keep = halve(4, tp, keep, got)
    got = move(send, Z6)
    others = (q1, q2, q3)
    state = attend(tie(host, send), others, (0, 1), (kv_own, kv_core))
    got = tie(got, *state)
    send, keep = halve(2, tp, keep, got)
    got = move(send, Z2)
    kv_diag = move(tie(kv_adj, send), CORE)
    back = attend(tie(host, send), others, (2, 3), (kv_adj, kv_diag), state, end=True)
    got = tie(got, *back)
    half = (2 * ROWS, HD)
    send, total = glue(add_kernel, (), (keep, got), ((half, BF16), (half, F32)), "add")
    got = move(send, Z1)
    m2, m3 = move(tie(back[1], send), Y2), move(tie(back[2], send), Y3)
    piece, = glue(join_kernel, (), (total, got, line), (((PIECE, HD), BF16),), "join")
    got = move(piece, XFAR)
    m1 = move(tie(back[0], piece), Y1)
    state = attend(tie(host, piece), (q_own,), (0, 1), (kv_own, kv_core))
    got = tie(got, m1, m2, m3, *state)
    pair, = glue(pair_kernel, (), (piece, got), (((PAIR, HD), BF16),), "pair")
    g2, g1, g3 = move(pair, Y2), move(pair, Y1), move(pair, Y3)
    mine, = attend(tie(host, pair), (q_own,), (2, 3), (kv_adj, kv_diag), state, end=True)
    near, = glue(near_kernel, (), (pair, g1, g2, tie(g3, mine)), (((4 * PAIR, HD), BF16),), "near")
    far = move(near, CORE)
    out_d, value, level = last_call(
        middle_kernel, (q_own, mine, m1, m2, m3, near, own_kv, pos),
        [((DROWS, HEADS * HD), BF16), ((PR, HD), F32), ((PR, HD), F32)], "middle",
    )
    far = tie(far, level)
    out_p, = last_call(
        final_kernel, (q_own, far, value, level, pos), [((ROWS, HEADS * HD), BF16)], "final"
    )
    return out_p, out_d


def solution(mesh):
    in_specs = (
        P("ctx", "tp"), P("tp", None), P("ctx", None), P("ctx", None), P("ctx", "tp"),
        P("ctx", "tp"), P("ctx", None), P("ctx", None), P("ctx"), P("ctx"), P("ctx"),
    )
    out_specs = (P("ctx", "tp"), P("ctx", "tp"))
    return jax.shard_map(body, mesh=mesh, in_specs=in_specs, out_specs=out_specs, check_vma=False)
```

```python
import functools
import math

import jax
import jax.numpy as jnp
from jax import lax
from jax.experimental import pallas as pl
from jax.experimental.pallas import tpu as pltpu
from jax.sharding import PartitionSpec as P

HD = 128
HEADS = 8
KVH = 8
ROWS = 64
DROWS = 8
PR = HEADS * ROWS
QR = PR + HEADS * DROWS
MSG = QR + 16
SLOTS = 1024
CHUNK = 256
EXP = HD ** -0.5 * math.log2(math.e)
MASKED = -1e30
FLOOR = -1e20
BASE = 32
F32 = jnp.float32
BF16 = jnp.bfloat16


def swap(f):
    out = []
    for i in range(256):
        y, xh, core, xl, z = i // 64, i // 32 % 2, i // 16 % 2, i // 8 % 2, i % 8
        y, xh, core, xl, z = f(y, xh, core, xl, z)
        out.append((i, (((y * 2 + xh) * 2 + core) * 2 + xl) * 8 + z))
    return out


CORE = swap(lambda y, xh, c, xl, z: (y, xh, 1 - c, xl, z))
XADJ = swap(lambda y, xh, c, xl, z: (y, 1 - xh, c, 1 - xl, z))
XFAR = swap(lambda y, xh, c, xl, z: (y, 1 - xh, c, xl, z))
XLOW = swap(lambda y, xh, c, xl, z: (y, xh, c, 1 - xl, z))
Y1, Y2, Y3 = (swap(lambda y, xh, c, xl, z, k=k: (y ^ k, xh, c, xl, z)) for k in (1, 2, 3))
Z1, Z2, Z6 = (swap(lambda y, xh, c, xl, z, k=k: (y, xh, c, xl, z ^ k)) for k in (1, 2, 6))


def tie(x, *others):
    return lax.optimization_barrier((x, *others))[0]


def move(x, pairs):
    return lax.ppermute(x, ("ctx", "tp"), pairs)


LIGHT = pl.CostEstimate(flops=1, bytes_accessed=1, transcendentals=0)


def vmem(mib):
    return pltpu.CompilerParams(vmem_limit_bytes=mib * 1024 * 1024)


PARTS = 4
KV = 2 * SLOTS + 16
PIECE = 2 * ROWS + 16
PAIR = 2 * PIECE


def project_kernel(tp, h, w, send, keep, acc):
    side = tp[0] // 8
    deep = h.shape[1] // PARTS
    for i in range(PARTS):
        part = slice(i * deep, (i + 1) * deep)
        product = jnp.dot(h[:, part], w[part, :], preferred_element_type=F32)
        acc[...] = product if i == 0 else acc[...] + product
    for i in range(4):
        for out, where in ((send, 1 - side), (keep, side)):
            at = (where * 4 + i) * HD
            for v in range(2):
                block = acc[:, pl.ds(pl.multiple_of(at + v * KVH * HD, HD), HD)]
                out[i, v * ROWS:(v + 1) * ROWS, :] = block.astype(out.dtype)


def far_call(kernel, scalars, arrays, outs, scratch, name):
    whole = pl.BlockSpec(memory_space=pltpu.VMEM)
    return pl.pallas_call(
        kernel,
        in_specs=[pl.BlockSpec(memory_space=pltpu.SMEM)] * len(scalars)
        + [pl.BlockSpec(memory_space=pl.ANY)] * len(arrays),
        out_specs=[whole] * len(outs),
        out_shape=[jax.ShapeDtypeStruct(shape, dtype) for shape, dtype in outs],
        scratch_shapes=scratch,
        compiler_params=vmem(12),
        cost_estimate=LIGHT,
        name=name,
    )(*scalars, *[pltpu.with_memory_space_constraint(x, pltpu.HBM) for x in arrays])


def project(tp, hidden, weight):
    half = (4, 2 * ROWS, HD)
    whole = pl.BlockSpec(memory_space=pltpu.VMEM)
    return pl.pallas_call(
        project_kernel,
        in_specs=[pl.BlockSpec(memory_space=pltpu.SMEM), whole, whole],
        out_specs=[whole, whole],
        out_shape=[jax.ShapeDtypeStruct(half, BF16), jax.ShapeDtypeStruct(half, F32)],
        scratch_shapes=[pltpu.VMEM((ROWS, weight.shape[1]), F32)],
        compiler_params=vmem(8),
        name="project",
    )(tp, hidden, weight)


def pack_kernel(
    tp, lengths, owner, pos, cache_k, cache_v, prompt_q, dec_q, dec_k, dec_v,
    kv_own, kv_give, q_own, own_kv, pos_line, pos_column,
    c, pq, dq, dkv, owner_s, pos_s, sem_c, sem_s,
):
    head = tp[0] // 2
    own = pl.ds(pl.multiple_of(head * HD, HD), HD)
    other = pl.ds(pl.multiple_of((head ^ 4) * HD, HD), HD)
    copy = pltpu.make_async_copy
    copies = [
        copy(source, target, sem_s.at[i])
        for i, (source, target) in enumerate((
            (owner, owner_s), (pos, pos_s), (prompt_q, pq), (dec_q, dq),
            (dec_k.at[:, own], dkv.at[0]), (dec_v.at[:, own], dkv.at[1]),
        ))
    ]
    copies_c = [
        copy(source.at[:, part], c.at[i], sem_c.at[i])
        for i, (source, part) in enumerate(
            ((cache_k, other), (cache_v, other), (cache_k, own), (cache_v, own))
        )
    ]
    for x in copies + copies_c:
        x.start()
    for x in copies:
        x.wait()
    for j in range(HEADS):
        q_own[j * ROWS:(j + 1) * ROWS, :] = pq[:, j * HD:(j + 1) * HD]
    d = dq[...].astype(F32)
    rows = jnp.concatenate([d[:, j * HD:(j + 1) * HD] for j in range(HEADS)], 0)
    q_own[PR:QR, :] = rows.astype(BF16)
    row = lax.broadcasted_iota(jnp.int32, (16, HD), 0)
    who = jnp.zeros((16, HD), jnp.int32)
    for r in range(DROWS):
        who = jnp.where(row == r, owner_s[r], who)
    q_own[QR:MSG, :] = who.astype(F32).astype(BF16)
    lane = lax.broadcasted_iota(jnp.int32, (16, HD), 1) % ROWS
    eight = lax.broadcasted_iota(jnp.int32, (DROWS, HD), 0)
    line = jnp.zeros((16, HD), jnp.int32)
    for b in range(ROWS // DROWS):
        column = jnp.zeros((DROWS, HD), jnp.int32)
        for r in range(DROWS):
            column = jnp.where(eight == r, pos_s[b * DROWS + r], column)
            line = jnp.where(lane == b * DROWS + r, pos_s[b * DROWS + r], line)
        pos_column[b * DROWS:(b + 1) * DROWS, :] = column.astype(F32)
    line = jnp.where(row == 0, line // BASE, jnp.where(row == 1, line % BASE, 0))
    pos_line[...] = line.astype(F32).astype(BF16)
    own_kv[0:DROWS, :] = dkv[0].astype(F32)
    own_kv[DROWS:2 * DROWS, :] = dkv[1].astype(F32)

    n = lengths[0]
    value = jnp.where(row < 8, n // BASE, n % BASE).astype(F32).astype(BF16)
    filled = lax.broadcasted_iota(jnp.int32, (SLOTS, HD), 0) < n
    for i, out in enumerate((kv_give, kv_own)):
        copies_c[2 * i].wait()
        copies_c[2 * i + 1].wait()
        keys = c[2 * i].astype(F32)
        out[0:SLOTS, :] = jnp.where(filled, keys, keys[0:1]).astype(BF16)
        out[SLOTS:2 * SLOTS, :] = jnp.where(filled, c[2 * i + 1].astype(F32), 0.0).astype(BF16)
        out[2 * SLOTS:KV, :] = value


def pack(tp, lengths, *arrays):
    outs = [((KV, HD), BF16), ((KV, HD), BF16), ((MSG, HD), BF16), ((2 * DROWS, HD), F32), ((16, HD), BF16), ((ROWS, HD), F32)]
    scratch = [
        pltpu.VMEM((4, SLOTS, HD), BF16),
        pltpu.VMEM((ROWS, HEADS * HD), BF16),
        pltpu.VMEM((DROWS, HEADS * HD), BF16),
        pltpu.VMEM((2, DROWS, HD), BF16),
        pltpu.SMEM((DROWS,), jnp.int32),
        pltpu.SMEM((ROWS,), jnp.int32),
        pltpu.SemaphoreType.DMA((4,)),
        pltpu.SemaphoreType.DMA((6,)),
    ]
    return far_call(pack_kernel, (tp, lengths), arrays, outs, scratch, "pack")


def glue(kernel, scalars, arrays, outs, name):
    whole = pl.BlockSpec(memory_space=pltpu.VMEM)
    return pl.pallas_call(
        kernel,
        in_specs=[pl.BlockSpec(memory_space=pltpu.SMEM)] * len(scalars) + [whole] * len(arrays),
        out_specs=[whole] * len(outs),
        out_shape=[jax.ShapeDtypeStruct(shape, dtype) for shape, dtype in outs],
        compiler_params=vmem(4),
        cost_estimate=LIGHT,
        name=name,
    )(*scalars, *arrays)


def halve_kernel(bit, tp, keep, got, send, left):
    half = send.shape[0]
    mine = tp[0] // bit % 2
    for i in range(half):
        j = (1 - mine) * half + i
        send[i] = (keep[j] + got[j].astype(F32)).astype(BF16)
        j = mine * half + i
        left[i] = keep[j] + got[j].astype(F32)


def halve(bit, tp, keep, got):
    shape = (keep.shape[0] // 2,) + keep.shape[1:]
    return glue(functools.partial(halve_kernel, bit), (tp,), (keep, got), ((shape, BF16), (shape, F32)), "halve")


def add_kernel(keep, got, send, total):
    x = keep[0] + got[0].astype(F32)
    send[...] = x.astype(BF16)
    total[...] = x


def join_kernel(total, got, line, piece):
    piece[0:2 * ROWS, :] = (total[...] + got[...].astype(F32)).astype(BF16)
    piece[2 * ROWS:PIECE, :] = line[...]


def pair_kernel(piece, got, out):
    out[0:PIECE, :] = piece[...]
    out[PIECE:PAIR, :] = got[...]


def near_kernel(pair, g1, g2, g3, out):
    for i, m in enumerate((pair, g1, g2, g3)):
        out[i * PAIR:(i + 1) * PAIR, :] = m[...]


BLOCK = 192
BATCH = 5


def absorb(ctx, n, kv, qs, acc, top):
    tail = kv[2 * SLOTS:2 * SLOTS + 16, :].astype(F32)
    length = jnp.max(tail[:8] * BASE + tail[8:]).astype(jnp.int32)
    host = (ctx[0] ^ n).astype(F32)

    def chunk(base, size):
        k = kv[pl.ds(pl.multiple_of(base, 256), size), :]
        v = kv[pl.ds(pl.multiple_of(SLOTS + base, 256), size), :]
        one = lax.broadcasted_iota(jnp.int32, (size, HD), 0) < length - base
        v = jnp.concatenate([v, jnp.where(one, 1.0, 0.0).astype(BF16)], 1)
        blocks = [(g, q, start) for g, q in enumerate(qs) for start in range(0, QR, BLOCK)]
        for first in range(0, len(blocks), BATCH):
            batch = blocks[first:first + BATCH]
            scores = [
                lax.dot_general(
                    q[start:start + BLOCK, :], k, (((1,), (1,)), ((), ())), preferred_element_type=F32
                )
                for g, q, start in batch
            ]
            weights = []
            for (g, q, start), s in zip(batch, scores):
                rows = slice(g * QR + start, g * QR + start + BLOCK)
                old = top[rows, :]
                new = jnp.maximum(old, jnp.max(s, axis=1, keepdims=True))
                less = new
                if start + BLOCK > PR:
                    owner = q[QR:MSG, :].astype(F32)[:DROWS]
                    owner = jnp.concatenate([jnp.full((BLOCK - QR + PR, HD), 99.0)] + [owner] * HEADS, 0)
                    seen = owner >= host
                    new = jnp.where(seen, new, old)
                    less = jnp.where(seen, new, -MASKED)
                p = jnp.exp2((s - jnp.concatenate([less] * (size // HD), 1)) * EXP)
                shrink = jnp.exp2((old - new) * EXP)
                top[rows, :] = new
                weights.append((rows, p.astype(BF16), shrink))
            for rows, p, shrink in weights:
                acc[rows, :] = acc[rows, :] * jnp.concatenate([shrink, shrink], 1) + jnp.dot(
                    p, v, preferred_element_type=F32
                )

    rest = length % 512
    full = length // 512 + (rest > 256).astype(jnp.int32)

    def step(c, carry):
        chunk(c * 512, 512)
        return carry

    lax.fori_loop(0, full, step, 0)

    @pl.when((rest > 0) & (rest <= 256))
    def _():
        chunk(full * 512, 256)


def attend_kernel(ctx, *refs, groups, hosts, begin, end):
    qs, kvs, refs = refs[:groups], refs[groups:groups + len(hosts)], refs[groups + len(hosts):]
    before, refs = ((), refs) if begin else (refs[:2], refs[2:])
    outs, (acc, top) = refs[:-2], refs[-2:]
    acc[...] = jnp.zeros_like(acc) if begin else before[0][...]
    top[...] = jnp.full_like(top, FLOOR) if begin else before[1][...]
    for n, kv in zip(hosts, kvs):
        absorb(ctx, n, kv, qs, acc, top)
    if not end:
        return
    diagonal = lax.broadcasted_iota(jnp.int32, (HD, HD), 0) == lax.broadcasted_iota(jnp.int32, (HD, HD), 1)
    index = lax.broadcasted_iota(jnp.int32, (16, HD), 0)
    for g, out in enumerate(outs):
        rows = slice(g * QR, (g + 1) * QR)
        total = acc[rows, HD:]
        out[0:QR, :] = (acc[rows, :HD] / jnp.where(total > 0.0, total, 1.0)).astype(BF16)
        packed = jnp.zeros((16, HD), F32)
        for b in range(5):
            low = g * QR + b * HD
            lines = []
            for ref, column in ((acc, HD), (top, 0)):
                block = ref[low:low + min(HD, QR - b * HD), column:column + HD]
                if b == 4:
                    block = jnp.concatenate([block, jnp.zeros((HD - QR + PR, HD), F32)], 0)
                lines.append(jnp.sum(jnp.where(diagonal, block, 0.0), axis=0, keepdims=True))
            some = lines[0] > 0.0
            line = jnp.where(some, lines[1] * EXP + jnp.log2(jnp.where(some, lines[0], 1.0)), FLOOR)
            for i in range(3):
                piece = line.astype(BF16).astype(F32)
                packed = jnp.where(index == 3 * b + i, piece, packed)
                line = line - piece
        out[QR:MSG, :] = packed.astype(BF16)


def attend(host, qs, hosts, kvs, state=(), end=False):
    whole = pl.BlockSpec(memory_space=pltpu.VMEM)
    shapes = ((len(qs) * QR, 2 * HD), (len(qs) * QR, HD))
    outs = [((MSG, HD), BF16)] * len(qs) if end else [(x, F32) for x in shapes]
    arrays = (*qs, *kvs, *state)
    return pl.pallas_call(
        functools.partial(attend_kernel, groups=len(qs), hosts=hosts, begin=not state, end=end),
        in_specs=[pl.BlockSpec(memory_space=pltpu.SMEM)] + [whole] * len(arrays),
        out_specs=[whole] * len(outs),
        out_shape=[jax.ShapeDtypeStruct(shape, dtype) for shape, dtype in outs],
        scratch_shapes=[pltpu.VMEM(shape, F32) for shape in shapes] if end else [],
        compiler_params=vmem(16),
        cost_estimate=LIGHT,
        name="attend",
    )(host, *arrays)


NEAR = 8


def lay_out(ref, keys, vals):
    vals[:, HD:] = jnp.ones((NEAR * ROWS, HD), BF16)
    lane = lax.broadcasted_iota(jnp.int32, (1, HD), 1)
    lines = []
    for i in range(NEAR):
        at = i * ROWS
        base = i * PIECE
        keys[at:at + ROWS, :] = ref[base:base + ROWS, :]
        vals[at:at + ROWS, 0:HD] = ref[base + ROWS:base + 2 * ROWS, :]
        tail = ref[base + 2 * ROWS:base + PIECE, :].astype(F32)
        lines.append(tail[0:1] * BASE + tail[1:2])
    return jnp.concatenate(
        [jnp.where(lane < ROWS, lines[2 * i], lines[2 * i + 1]) for i in range(NEAR // 2)], 1
    )


def prompt_part(q, mask, keys, vals):
    s = lax.dot_general(q, keys[...], (((1,), (1,)), ((), ())), preferred_element_type=F32)
    s = jnp.where(mask, s, MASKED)
    high = jnp.maximum(jnp.max(s, axis=1, keepdims=True), FLOOR)
    p = jnp.exp2((s - high) * EXP)
    o = jnp.dot(p.astype(BF16), vals[...], preferred_element_type=F32)
    return high * EXP, o[:, HD:], o[:, :HD]


def middle_kernel(q, m0, m1, m2, m3, near, own_kv, pos, out_d, value, level, keys, vals):
    parts = ((m0, 0), (m1, 0), (m2, 0), (m3, 0))
    where = lay_out(near, keys, vals)
    diagonal = lax.broadcasted_iota(jnp.int32, (HD, HD), 0) == lax.broadcasted_iota(jnp.int32, (HD, HD), 1)

    def column(ref, base, b):
        tail = ref[base + QR:base + MSG, :].astype(F32)
        line = tail[3 * b:3 * b + 1] + tail[3 * b + 1:3 * b + 2] + tail[3 * b + 2:3 * b + 3]
        return jnp.sum(jnp.where(diagonal, line, 0.0), axis=1, keepdims=True)

    def merge(b, size, top, total, summed):
        tops = [column(ref, base, b)[:size] for ref, base in parts]
        high = functools.reduce(jnp.maximum, tops, top)
        weight = jnp.exp2(top - high)
        summed, total = weight * summed, weight * total
        for x, (ref, base) in zip(tops, parts):
            weight = jnp.exp2(x - high)
            summed = summed + weight * ref[base + b * HD:base + b * HD + size, :].astype(F32)
            total = total + weight
        return summed / total, high + jnp.log2(total)

    mine = jnp.concatenate([pos[...], pos[...]], 0)[:, 0:1]
    mask = where <= mine
    for b in range(4):
        rows = slice(b * HD, (b + 1) * HD)
        got, high = merge(b, HD, *prompt_part(q[rows, :], mask, keys, vals))
        value[rows, :] = got
        level[rows, :] = high
    key = jnp.concatenate([own_kv[0:DROWS, :]] * HEADS, 0)
    own = jnp.concatenate([own_kv[DROWS:2 * DROWS, :]] * HEADS, 0)
    top = jnp.sum(q[PR:QR, :].astype(F32) * key, axis=1, keepdims=True) * EXP
    got, high = merge(4, QR - PR, top, jnp.ones((QR - PR, HD), F32), own)
    for j in range(HEADS):
        out_d[:, j * HD:(j + 1) * HD] = got[j * DROWS:(j + 1) * DROWS].astype(BF16)


def final_kernel(q, far, value, level, pos, out_p, keys, vals):
    where = lay_out(far, keys, vals)
    mine = jnp.concatenate([pos[...], pos[...]], 0)[:, 0:1]
    mask = where <= mine
    for b in range(4):
        rows = slice(b * HD, (b + 1) * HD)
        top, total, summed = prompt_part(q[rows, :], mask, keys, vals)
        before = level[rows, :]
        high = jnp.maximum(top, before)
        left, right = jnp.exp2(before - high), jnp.exp2(top - high)
        merged = ((left * value[rows, :] + right * summed) / (left + right * total)).astype(BF16)
        out_p[:, 2 * b * HD:(2 * b + 1) * HD] = merged[:ROWS]
        out_p[:, (2 * b + 1) * HD:(2 * b + 2) * HD] = merged[ROWS:]


def last_call(kernel, arrays, outs, name):
    whole = pl.BlockSpec(memory_space=pltpu.VMEM)
    return pl.pallas_call(
        kernel,
        in_specs=[whole] * len(arrays),
        out_specs=[whole] * len(outs),
        out_shape=[jax.ShapeDtypeStruct(shape, dtype) for shape, dtype in outs],
        scratch_shapes=[pltpu.VMEM((NEAR * ROWS, HD), BF16), pltpu.VMEM((NEAR * ROWS, 2 * HD), BF16)],
        compiler_params=vmem(8),
        cost_estimate=LIGHT,
        name=name,
    )(*arrays)


def body(
    prompt_hidden, kv_weight, cache_k, cache_v, prompt_q, dec_q, dec_k, dec_v,
    cache_lengths, prompt_pos, dec_owner,
):
    host = lax.axis_index("ctx").reshape(1)
    tp = lax.axis_index("tp").reshape(1)
    send, keep = project(tp, prompt_hidden, kv_weight)
    kv_own, kv_give, q_own, own_kv, line, pos = pack(
        tp, cache_lengths, dec_owner, prompt_pos, cache_k, cache_v, prompt_q, dec_q, dec_k, dec_v
    )
    kv_adj = move(kv_give, XADJ)
    kv_core = move(kv_own, CORE)
    got = move(tie(send, kv_core), XLOW)
    q1 = move(q_own, Y1)
    q2, q3 = move(q_own, Y2), move(q_own, Y3)

    send, keep = halve(4, tp, keep, got)
    got = move(send, Z6)
    others = (q1, q2, q3)
    state = attend(tie(host, send), others, (0, 1), (kv_own, kv_core))
    got = tie(got, *state)
    send, keep = halve(2, tp, keep, got)
    got = move(send, Z2)
    kv_diag = move(tie(kv_adj, send), CORE)
    back = attend(tie(host, send), others, (2, 3), (kv_adj, kv_diag), state, end=True)
    got = tie(got, *back)
    half = (2 * ROWS, HD)
    send, total = glue(add_kernel, (), (keep, got), ((half, BF16), (half, F32)), "add")
    got = move(send, Z1)
    m3, m2 = move(tie(back[2], send), Y3), move(tie(back[1], send), Y2)
    piece, = glue(join_kernel, (), (total, got, line), (((PIECE, HD), BF16),), "join")
    got = move(piece, XFAR)
    m1 = move(tie(back[0], piece), Y1)
    state = attend(tie(host, piece), (q_own,), (0, 1), (kv_own, kv_core))
    got = tie(got, m3, m1, m2, *state)
    pair, = glue(pair_kernel, (), (piece, got), (((PAIR, HD), BF16),), "pair")
    g2, g1, g3 = move(pair, Y2), move(pair, Y1), move(pair, Y3)
    mine, = attend(tie(host, pair), (q_own,), (2, 3), (kv_adj, kv_diag), state, end=True)
    near, = glue(near_kernel, (), (pair, g1, g2, tie(g3, mine)), (((4 * PAIR, HD), BF16),), "near")
    far = move(near, CORE)
    out_d, value, level = last_call(
        middle_kernel, (q_own, mine, m1, m2, m3, near, own_kv, pos),
        [((DROWS, HEADS * HD), BF16), ((PR, HD), F32), ((PR, HD), F32)], "middle",
    )
    far = tie(far, level)
    out_p, = last_call(
        final_kernel, (q_own, far, value, level, pos), [((ROWS, HEADS * HD), BF16)], "final"
    )
    return out_p, out_d


def solution(mesh):
    in_specs = (
        P("ctx", "tp"), P("tp", None), P("ctx", None), P("ctx", None), P("ctx", "tp"),
        P("ctx", "tp"), P("ctx", None), P("ctx", None), P("ctx"), P("ctx"), P("ctx"),
    )
    out_specs = (P("ctx", "tp"), P("ctx", "tp"))
    return jax.shard_map(body, mesh=mesh, in_specs=in_specs, out_specs=out_specs, check_vma=False)
```
